512 devices in a mesh: prompt: 16 (over z), seq: 32 (over y, x, core).
Axes of the slice: x: 4, y: 4, z: 16, core: 2. Of those that a mesh axis runs over, the one named last changes fastest.
Arguments:
- queries: bfloat16 [16, 32, 2, 32, 128], P('prompt', 'seq'), may hold values from -160 to 160
- prompt_key_cache: bfloat16 [16, 4, 8192, 128], P('prompt', None, 'seq'), may hold values from -5 to 5
- prompt_value_cache: bfloat16 [16, 4, 8192, 128], P('prompt', None, 'seq'), may hold values from -6 to 6
- kept: int32 [16, 4, 32], P('prompt', None, 'seq'), may hold values from 1 to 2, as said below
- sample_keys: bfloat16 [16, 32, 4, 256, 128], P('prompt', 'seq'), may hold values from -6 to 6
- sample_values: bfloat16 [16, 32, 4, 256, 128], P('prompt', 'seq'), may hold values from -6 to 6
- suffix_len: int32 [16, 32], P('prompt', 'seq'), may hold values from 1 to 256, as said below
- decode_keys: bfloat16 [16, 32, 2, 4, 128], P('prompt', 'seq'), may hold values from -6 to 6
- decode_values: bfloat16 [16, 32, 2, 4, 128], P('prompt', 'seq'), may hold values from -6 to 6
- out_weight: bfloat16 [4096, 8192], P('seq', 'prompt'), may hold values from -0.1875 to 0.1875
Outputs:
- attn_out: bfloat16 [1024, 8192], P('seq', 'prompt')
The draws below stay inside these ranges and needn't reach their ends.
Inputs may be any that keep to these rules, and one draw needn't show every extreme that they name: `kept`: for every prompt and key-value head some seq index has all 2 slots live. `suffix_len`: in every prompt some sample has 256 generated tokens.
All inputs are finite; a program needn't handle non-finite values.
Results may differ from the reference program's by a relative error of at most 0.0048.
Values may be sent and summed in bfloat16 or wider, within the bound.
A program may use at most 128 MiB of HBM per device.

```python
import math
import jax
import jax.numpy as jnp
from jax import lax

D = 8192
KEY_VALUE_HEADS = 4
QUERY_GROUP = 8
HEAD_SIZE = 128
BLOCK_TOKENS = 128
DECODE_STEPS = 2
KEPT_SLOTS = 2
SUFFIX_LENGTH = 256
HQ = 32
PROMPT_COUNT = 16
SAMPLE_COUNT = 32
PROMPT_LENGTH = 8192
ROWS = 1024
N_SEQ = 32


def joint_draw(key):
    base_offset = jax.random.fold_in(key, 101)
    key_layout = (PROMPT_COUNT, KEY_VALUE_HEADS, N_SEQ * KEPT_SLOTS * BLOCK_TOKENS, HEAD_SIZE)
    query_shape = (PROMPT_COUNT, SAMPLE_COUNT, DECODE_STEPS, HQ, HEAD_SIZE)
    scale_shape = (PROMPT_COUNT, SAMPLE_COUNT, DECODE_STEPS, HQ, 1)
    row_scale = jnp.exp(jax.random.uniform(jax.random.fold_in(base_offset, 5), scale_shape, jnp.float32, math.log(2.5), math.log(15.0)))
    key_cache_store = jnp.clip(jax.random.normal(jax.random.fold_in(base_offset, 1), key_layout, jnp.float32), -5.0, 5.0)
    query_tile_block = row_scale * jnp.clip(jax.random.normal(jax.random.fold_in(base_offset, 2), query_shape, jnp.float32), -6.0, 6.0)
    return (key_cache_store, query_tile_block)


def draw_queries(key, part):
    return joint_draw(key)[1].astype(jnp.bfloat16)


def draw_prompt_key_cache(key, part):
    return joint_draw(key)[0].astype(jnp.bfloat16)


def draw_kept(key, part):
    base_offset = jax.random.fold_in(key, 202)
    kept_block_counts = jax.random.randint(jax.random.fold_in(base_offset, 1), (PROMPT_COUNT, KEY_VALUE_HEADS, N_SEQ), 1, KEPT_SLOTS + 1)
    fullest_count = jax.random.randint(jax.random.fold_in(base_offset, 2), (PROMPT_COUNT, KEY_VALUE_HEADS), 0, N_SEQ)
    device_ids = jnp.arange(N_SEQ, dtype=jnp.int32)
    return jnp.where(device_ids[None, None, :] == fullest_count[:, :, None], KEPT_SLOTS, kept_block_counts).astype(jnp.int32)


def draw_suffix_len(key, part):
    base_offset = jax.random.fold_in(key, 303)
    lengths = jax.random.randint(jax.random.fold_in(base_offset, 1), (PROMPT_COUNT, SAMPLE_COUNT), 1, SUFFIX_LENGTH + 1)
    longest = jax.random.randint(jax.random.fold_in(base_offset, 2), (PROMPT_COUNT,), 0, SAMPLE_COUNT)
    sample_ids = jnp.arange(SAMPLE_COUNT, dtype=jnp.int32)
    return jnp.where(sample_ids[None, :] == longest[:, None], SUFFIX_LENGTH, lengths).astype(jnp.int32)


def shard_levels(stream_key, extent, split, least, top_value):
    factor_of, own = 1.0, jax.random.fold_in(stream_key, 6)
    for dim, blocks in split:
        heights = jnp.exp(jax.random.uniform(jax.random.fold_in(own, dim), (blocks,), jnp.float32, least / len(split), top_value / len(split)))
        factor_of = factor_of * jnp.repeat(heights, extent[dim] // blocks).reshape([-1 if axis == dim else 1 for axis in range(len(extent))])
    return factor_of


def scatter_about(own_key, extent, spread, bound, cuts=(), held_as=jnp.bfloat16):
    result = jax.random.normal(own_key, extent, jnp.float32) * spread
    if len(cuts) > 0:
        result = shard_levels(own_key, extent, cuts, -0.22, 0.18) * result
    return jnp.clip(result, min=-bound, max=bound).astype(held_as)


def setup_inputs(seed: int = 0) -> dict:
    streams_of = jax.random.split(jax.random.key(seed), 11)
    return {
        "queries": draw_queries(jax.random.fold_in(streams_of[10], 71), 0),
        "prompt_key_cache": draw_prompt_key_cache(jax.random.fold_in(streams_of[10], 71), 0),
        "prompt_value_cache": scatter_about(streams_of[2], (PROMPT_COUNT, KEY_VALUE_HEADS, PROMPT_LENGTH, HEAD_SIZE), 1.0, 6.0, ((0, 16), (2, 32))),
        "kept": draw_kept(jax.random.fold_in(streams_of[10], 71), 0),
        "sample_keys": scatter_about(streams_of[4], (PROMPT_COUNT, SAMPLE_COUNT, KEY_VALUE_HEADS, SUFFIX_LENGTH, HEAD_SIZE), 1.3, 6.0, ((0, 16), (1, 32))),
        "sample_values": scatter_about(streams_of[5], (PROMPT_COUNT, SAMPLE_COUNT, KEY_VALUE_HEADS, SUFFIX_LENGTH, HEAD_SIZE), 1.0, 6.0, ((0, 16), (1, 32))),
        "suffix_len": draw_suffix_len(jax.random.fold_in(streams_of[10], 71), 0),
        "decode_keys": scatter_about(streams_of[7], (PROMPT_COUNT, SAMPLE_COUNT, DECODE_STEPS, KEY_VALUE_HEADS, HEAD_SIZE), 1.3, 6.0, ((0, 16), (1, 32))),
        "decode_values": scatter_about(streams_of[8], (PROMPT_COUNT, SAMPLE_COUNT, DECODE_STEPS, KEY_VALUE_HEADS, HEAD_SIZE), 1.0, 6.0, ((0, 16), (1, 32))),
        "out_weight": scatter_about(streams_of[9], (HQ * HEAD_SIZE, D), (HQ * HEAD_SIZE // 4) ** -0.5, 0.1875, ((0, 32), (1, 16))),
    }


NEGATIVE = -1e+30

def rounded_length(values):
    return lax.optimization_barrier(values.astype(jnp.bfloat16)).astype(jnp.float32)

def reference(queries, prompt_key_cache, prompt_value_cache, kept, sample_keys, sample_values, suffix_len, decode_keys, decode_values, out_weight):
    logit_scale = 1.0 / math.sqrt(HEAD_SIZE)
    block_total = N_SEQ * KEPT_SLOTS

    def one_prompt(prompt_position):
        query_tile_block = queries[prompt_position].astype(jnp.float32)
        grouped_queries = query_tile_block.reshape(SAMPLE_COUNT, DECODE_STEPS, KEY_VALUE_HEADS, QUERY_GROUP, HEAD_SIZE)
        heads_leading = jnp.transpose(grouped_queries, (2, 0, 1, 3, 4)).reshape(KEY_VALUE_HEADS, SAMPLE_COUNT * DECODE_STEPS * QUERY_GROUP, HEAD_SIZE)
        key_cache_store = prompt_key_cache[prompt_position].astype(jnp.float32).reshape(KEY_VALUE_HEADS, block_total, BLOCK_TOKENS, HEAD_SIZE)
        value_cache_store = prompt_value_cache[prompt_position].astype(jnp.float32).reshape(KEY_VALUE_HEADS, block_total, BLOCK_TOKENS, HEAD_SIZE)
        slot_position = jnp.arange(KEPT_SLOTS, dtype=jnp.int32)
        active_mask = (slot_position[None, None, :] < kept[prompt_position][:, :, None]).reshape(KEY_VALUE_HEADS, block_total)

        def one_head(pieces):
            head_row_block, key_block_list, value_block_list, live_blocks = pieces
            logit_scores = jnp.einsum('eg,mxg->emx', head_row_block, key_block_list) * logit_scale
            block_max = jnp.where(live_blocks[None, :], lax.optimization_barrier(jnp.max(logit_scores, axis=2)), NEGATIVE)
            attention_weights = jnp.where(live_blocks[None, :, None], jnp.exp(logit_scores - block_max[:, :, None]), 0.0)
            block_sum = lax.optimization_barrier(jnp.sum(attention_weights, axis=2))
            block_output = jnp.einsum('yaf,afi->yai', rounded_length(attention_weights), value_block_list)
            highest = lax.optimization_barrier(jnp.max(block_max, axis=1))
            factor = jnp.exp(block_max - highest[:, None])
            return (highest, lax.optimization_barrier(jnp.sum(factor * block_sum, axis=1)), lax.optimization_barrier(jnp.sum(factor[:, :, None] * block_output, axis=1)))
        prompt_maximum, prompt_sum, prompt_output = lax.map(one_head, (heads_leading, key_cache_store, value_cache_store, active_mask))
        suffix_keys = sample_keys[prompt_position].astype(jnp.float32)
        fresh_keys = jnp.transpose(decode_keys[prompt_position].astype(jnp.float32), (0, 2, 1, 3))
        all_keys = jnp.concatenate([suffix_keys, fresh_keys], axis=2)
        suffix_values = sample_values[prompt_position].astype(jnp.float32)
        fresh_values = jnp.transpose(decode_values[prompt_position].astype(jnp.float32), (0, 2, 1, 3))
        all_values = jnp.concatenate([suffix_values, fresh_values], axis=2)
        logit_scores = jnp.einsum('nthgd,nhid->nhtgi', grouped_queries, all_keys) * logit_scale
        position = jnp.arange(SUFFIX_LENGTH, dtype=jnp.int32)
        sample_token_mask = position[None, :] < suffix_len[prompt_position][:, None]
        sample_token_mask = jnp.broadcast_to(sample_token_mask[:, None, None, None, :], (SAMPLE_COUNT, KEY_VALUE_HEADS, DECODE_STEPS, QUERY_GROUP, SUFFIX_LENGTH))
        step_index = jnp.arange(DECODE_STEPS, dtype=jnp.int32)
        newest_token_mask = step_index[None, :] <= step_index[:, None]
        newest_token_mask = jnp.broadcast_to(newest_token_mask[None, None, :, None, :], (SAMPLE_COUNT, KEY_VALUE_HEADS, DECODE_STEPS, QUERY_GROUP, DECODE_STEPS))
        full_mask = jnp.concatenate([sample_token_mask, newest_token_mask], axis=4)
        tail_max = lax.optimization_barrier(jnp.max(jnp.where(full_mask, logit_scores, NEGATIVE), axis=4))
        attention_weights = jnp.where(full_mask, jnp.exp(logit_scores - tail_max[..., None]), 0.0)
        tail_sum = lax.optimization_barrier(jnp.sum(attention_weights, axis=4))
        tail_out = jnp.einsum('nhtgi,nhid->nhtgd', rounded_length(attention_weights), all_values)
        prefix_maximum = jnp.transpose(prompt_maximum.reshape(KEY_VALUE_HEADS, SAMPLE_COUNT, DECODE_STEPS, QUERY_GROUP), (1, 0, 2, 3))
        prefix_total_sum = jnp.transpose(prompt_sum.reshape(KEY_VALUE_HEADS, SAMPLE_COUNT, DECODE_STEPS, QUERY_GROUP), (1, 0, 2, 3))
        prefix_output = jnp.transpose(prompt_output.reshape(KEY_VALUE_HEADS, SAMPLE_COUNT, DECODE_STEPS, QUERY_GROUP, HEAD_SIZE), (1, 0, 2, 3, 4))
        highest = jnp.maximum(prefix_maximum, tail_max)
        prefix_factor = jnp.exp(prefix_maximum - highest)
        tail_factor = jnp.exp(tail_max - highest)
        softmax_total = prefix_total_sum * prefix_factor + tail_sum * tail_factor
        summed = prefix_output * prefix_factor[..., None] + tail_out * tail_factor[..., None]
        head_values = summed / softmax_total[..., None]
        head_values = jnp.transpose(head_values, (0, 2, 1, 3, 4)).reshape(SAMPLE_COUNT * DECODE_STEPS, HQ * HEAD_SIZE)
        return head_values.astype(jnp.bfloat16)
    head_outputs = lax.map(one_prompt, jnp.arange(PROMPT_COUNT, dtype=jnp.int32))
    flat_rows = head_outputs.reshape(ROWS, HQ * HEAD_SIZE)
    part_width = HQ * HEAD_SIZE // N_SEQ

    def add_group(running, group_index):
        part_rows = lax.dynamic_slice_in_dim(flat_rows, group_index * part_width, part_width, 1)
        part_weight = lax.dynamic_slice_in_dim(out_weight, group_index * part_width, part_width, 0)
        partial_value = jnp.dot(part_rows, part_weight, preferred_element_type=jnp.float32)
        return (running + partial_value, None)
    running, unused = lax.scan(add_group, jnp.zeros((ROWS, D), jnp.float32), jnp.arange(N_SEQ, dtype=jnp.int32))
    return running.astype(jnp.bfloat16)
```

```python
import functools
import math

import jax
import jax.numpy as jnp
from jax import lax
from jax.experimental import pallas as pl
from jax.experimental.pallas import tpu as pltpu
from jax.sharding import PartitionSpec as P

MESH = pl.DeviceIdType.MESH
bf16 = jnp.bfloat16
f32 = jnp.float32
NEGATIVE = -1e30

NP = 16
NS = 32
SCALE = 1.0 / math.sqrt(128)
FAR, NEAR = (6, -6, 3, -3), (1, -1)
HOPS = sorted(
    ((dy, dx) for dy in range(4) for dx in range(4)),
    key=lambda t: -(min(t[0], 4 - t[0]) + min(t[1], 4 - t[1])),
)
NT = (((1,), (1,)), ((), ()))
TN = (((0,), (0,)), ((), ()))


def dot(a, b, dims=(((1,), (0,)), ((), ()))):
    return lax.dot_general(a, b, dims, preferred_element_type=f32)


def iota(shape, axis):
    return lax.broadcasted_iota(jnp.int32, shape, axis)


def kernel(
    q_ref, k_ref, v_ref, kept_ref, sk_ref, sv_ref, len_ref, dk_ref, dv_ref, w_ref,
    out_ref,
    qv, qsend, qbuf, kbuf, vbuf, vt, skv, svv, dkv, dvv, flag_out, flag, qpl,
    tail_out, tail, part, rbuf, zbuf, wbuf, psend, obuf,
    lsem, ssem, rsem, zssem, zrsem,
):
    p, s = lax.axis_index("prompt"), lax.axis_index("seq")
    y, i = lax.div(s, 8), lax.rem(s, 8)
    x, c = lax.div(i, 2), lax.rem(s, 2)
    chip, other = lax.div(s, 2), 1 - c
    sib = s + 1 - 2 * c

    def at(plane, seq):
        return {"prompt": plane, "seq": seq}

    def zoff(o):
        return lax.rem(p + o + NP, NP)

    def remote(src, dst, send, recv, plane, seq):
        return pltpu.make_async_remote_copy(
            src, dst, send, recv, device_id=at(plane, seq), device_id_type=MESH
        )

    def wait_bytes(ref, sem):
        pltpu.make_async_copy(ref, ref, sem).wait()

    def send_or_keep(src, dst, n, seq):
        own = seq == s

        @pl.when(own)
        def _():
            pltpu.make_async_copy(src, dst, rsem.at[n]).start()

        @pl.when(jnp.logical_not(own))
        def _():
            remote(src, dst, ssem.at[n], rsem.at[n], p, seq).start()

    local = [
        pltpu.make_async_copy(q_ref.at[0, 0], qv, lsem.at[0]),
        pltpu.make_async_copy(sk_ref.at[0, 0], skv, lsem.at[1]),
        pltpu.make_async_copy(dk_ref.at[0, 0], dkv, lsem.at[2]),
        pltpu.make_async_copy(sv_ref.at[0, 0], svv, lsem.at[3]),
        pltpu.make_async_copy(dv_ref.at[0, 0], dvv, lsem.at[4]),
        pltpu.make_async_copy(k_ref.at[0, pl.ds(2 * c, 2)], kbuf.at[c], lsem.at[5]),
        pltpu.make_async_copy(v_ref.at[0, pl.ds(2 * c, 2)], vbuf.at[c], lsem.at[6]),
    ]
    for copy in local:
        copy.start()

    barrier = pltpu.get_barrier_semaphore()

    def greet(k, carry):
        pl.semaphore_signal(
            barrier, inc=1, device_id=at(p, lax.rem(s + k, NS)), device_id_type=MESH
        )
        return carry

    lax.fori_loop(1, NS, greet, 0)
    zpartners = (1, -1, 2, -2, 3, -3, 6, -6)
    for o in zpartners:
        pl.semaphore_signal(barrier, inc=1, device_id=at(zoff(o), s), device_id_type=MESH)

    local[0].wait()
    heads = qv[...].astype(f32).reshape(2, 4, 8, 128)
    for h in range(4):
        rows = heads[:, h].reshape(16, 128).astype(bf16)
        qsend[h] = rows
    row8 = iota((8, 128), 0)

    def flags(core):
        first = kept_ref[0, 2 * core, 0].astype(f32)
        second = kept_ref[0, 2 * core + 1, 0].astype(f32)
        return jnp.where(row8 == 0, first, second)

    flag[c] = flags(c)
    flag_out[...] = flags(other)

    pl.semaphore_wait(barrier, NS - 1 + len(zpartners))

    for dy, dx in HOPS:
        base = lax.rem(y + dy, 4) * 8 + lax.rem(x + dx, 4) * 2
        for core in range(2):
            if (dy, dx) != (0, 0):
                remote(
                    qsend.at[pl.ds(2 * core, 2)], qbuf.at[s], ssem.at[0], rsem.at[0], p, base + core
                ).start()
    remote(qsend.at[pl.ds(2 * other, 2)], qbuf.at[s], ssem.at[0], rsem.at[0], p, sib).start()
    pltpu.make_async_copy(qsend.at[pl.ds(2 * c, 2)], qbuf.at[s], rsem.at[0]).start()
    swap = [
        remote(k_ref.at[0, pl.ds(2 * other, 2)], kbuf.at[c], ssem.at[1], rsem.at[1], p, sib),
        remote(v_ref.at[0, pl.ds(2 * other, 2)], vbuf.at[c], ssem.at[2], rsem.at[2], p, sib),
        remote(flag_out, flag.at[c], ssem.at[3], rsem.at[3], p, sib),
    ]
    for copy in swap:
        copy.start()
    for dx in (2, 1, 3, 0):
        for half in range(2):
            send_or_keep(
                w_ref.at[pl.ds(64 * half, 64)], wbuf.at[i], 4, y * 8 + lax.rem(x + dx, 4) * 2 + half
            )

    lane = iota((1, 128), 1)
    qpl[...] = jnp.zeros((4, 128, 128), bf16)
    for h in range(4):
        qpl[h, pl.ds(pl.multiple_of(16 * i, 16), 16), :] = qsend[h]
    for copy in local[1:5]:
        copy.wait()
    placed = qpl[...].reshape(512, 128)
    fresh = [dot(dkv[u], placed, NT) * SCALE for u in range(2)]
    later_step = lax.rem(lax.div(lane, 8), 2) == 1
    key_mask = iota((256, 128), 0) < len_ref[0, 0]
    row16 = iota((16, 128), 0)
    for h in range(4):
        scores = dot(skv[h], qpl[h], NT) * SCALE
        scores = jnp.where(key_mask, scores, NEGATIVE)
        f0 = fresh[0][h : h + 1, 128 * h : 128 * h + 128]
        f1 = jnp.where(later_step, fresh[1][h : h + 1, 128 * h : 128 * h + 128], NEGATIVE)
        top = jnp.maximum(jnp.max(scores, axis=0, keepdims=True), jnp.maximum(f0, f1))
        e = jnp.where(key_mask, jnp.exp(scores - top), 0.0)
        e0, e1 = jnp.exp(f0 - top), jnp.where(later_step, jnp.exp(f1 - top), 0.0)
        total = jnp.sum(e, axis=0, keepdims=True) + e0 + e1
        value0 = dvv[0].astype(f32)[h : h + 1]
        value1 = dvv[1].astype(f32)[h : h + 1]
        values = jnp.where(row16 == 0, value0, jnp.where(row16 == 1, value1, 0.0)).astype(bf16)
        weights = jnp.where(row16 == 0, e0, jnp.where(row16 == 1, e1, 0.0)).astype(bf16)
        o = dot(svv[h], e.astype(bf16), TN) + dot(values, weights, TN)
        stats = jnp.where(row8 == 0, top, total)
        core, j = h // 2, h % 2

        @pl.when(c == core)
        def _():
            tail[c, j, :128] = o
            tail[c, j, 128:] = stats

        @pl.when(c != core)
        def _():
            tail_out[j, :128] = o
            tail_out[j, 128:] = stats

    tail_copy = remote(tail_out, tail.at[c], ssem.at[5], rsem.at[5], p, sib)
    tail_copy.start()

    local[5].wait()
    local[6].wait()
    for n in (1, 2, 3):
        swap[n - 1].wait_recv()
    for j in range(2):
        for core in range(2):
            vt[j, core] = jnp.transpose(vbuf[core, j])
    tail_copy.wait_recv()

    wait_bytes(qbuf, rsem.at[0])
    for kk in range(4):
        chunk = lax.rem(y + kk, 4)
        for j in range(2):
            rows = qbuf[pl.ds(8 * chunk, 8), j].reshape(128, 128)
            tops, sums, outs = [], [], []
            for core in range(2):
                scores = dot(kbuf[core, j], rows, NT) * SCALE
                for slot in range(2):
                    block = scores[128 * slot : 128 * slot + 128]
                    block_max = jnp.max(block, axis=0, keepdims=True)
                    e = jnp.exp(block - block_max)
                    sums.append(jnp.sum(e, axis=0, keepdims=True))
                    outs.append(dot(vt[j, core, :, 128 * slot : 128 * slot + 128], e.astype(bf16)))
                    if slot == 1:
                        live = flag[core, j : j + 1, :] > 1.5
                        block_max = jnp.where(live, block_max, NEGATIVE)
                    tops.append(block_max)
            if kk == 0:
                for core in range(2):
                    mine = lax.div(lane, 16) == 2 * x + core
                    tops.append(jnp.where(mine, tail[core, j, 128:129], NEGATIVE))
                    sums.append(tail[core, j, 129:130])
                    outs.append(tail[core, j, :128])
            top = functools.reduce(jnp.maximum, tops).astype(bf16).astype(f32)
            total, summed = 0.0, 0.0
            for m, t, o in zip(tops, sums, outs):
                factor = jnp.exp(m - top)
                total = total + factor * t
                summed = summed + factor * o
            high = total.astype(bf16).astype(f32)
            stats = jnp.where(row16 == 0, top, jnp.where(row16 == 1, high, total - high))
            stats = stats.astype(bf16)
            summed = summed.astype(bf16)
            for half in range(2):
                part[kk, j, half, :64] = summed[64 * half : 64 * half + 64]
                part[kk, j, half, 64:] = stats
                send_or_keep(
                    part.at[kk, j, half], rbuf.at[chip], 6, (2 * c + j) * 8 + chunk * 2 + half
                )

    wait_bytes(rbuf, rsem.at[6])
    tops = [rbuf[k, 64:80].astype(f32) for k in range(16)]
    top = functools.reduce(jnp.maximum, [t[0:1] for t in tops])
    total, summed = 0.0, 0.0
    for k in range(16):
        factor = jnp.exp(tops[k][0:1] - top)
        total = total + factor * (tops[k][1:2] + tops[k][2:3])
        summed = summed + factor * rbuf[k, :64].astype(f32)
    head_out = (summed / total).astype(bf16)
    blank = jnp.zeros_like(head_out)
    stacked = jnp.concatenate(
        [jnp.concatenate([head_out, blank], axis=1), jnp.concatenate([blank, head_out], axis=1)],
        axis=0,
    )
    a, b = iota((64, 256), 0), iota((64, 256), 1)
    wanted = lax.rem(a, 16) * 8 + 2 * lax.div(a, 16) + lax.div(b, 128)
    pick = jnp.where(lax.rem(b, 128) == wanted, 1.0, 0.0).astype(bf16)
    laid = dot(pick, stacked, NT).astype(bf16)
    for g in range(4):
        zbuf[p, :, 128 * g : 128 * g + 128] = laid[16 * g : 16 * g + 16]

    sends = []

    def zsend(src, dst, o):
        n = len(sends)
        copy = remote(src, dst, zssem.at[n], zrsem.at[n], zoff(o), s)
        copy.start()
        sends.append(copy)
        return copy

    first = [zsend(zbuf.at[p], zbuf.at[p], o) for o in FAR]
    second = [zsend(zbuf.at[p], zbuf.at[p], o) for o in NEAR]
    for o, copy in zip(FAR, first):
        copy.wait_recv()
        q = zoff(-o)
        if abs(o) == 6:
            lanes = pl.ds(0 if o > 0 else 256, 256)
            part_ref = zbuf.at[q, :, lanes]
            second.append(zsend(part_ref, part_ref, 2 if o > 0 else -2))
        for n in NEAR:
            second.append(zsend(zbuf.at[q], zbuf.at[q], n))
    for copy in second:
        copy.wait_recv()

    wait_bytes(wbuf, rsem.at[4])
    terms = dot(zbuf[...].reshape(256, 512), wbuf[...].reshape(512, 512))
    psend[...] = terms.astype(bf16).reshape(16, 16, 512)
    mine = lax.rem(x, 2) * 8 + 2 * y + c
    for dy, dx in HOPS:
        prompt = lax.rem(y + dy, 4) * 4 + lax.rem(x + dx, 4)
        send_or_keep(psend.at[prompt], obuf.at[mine], 7, 2 * prompt + lax.div(x, 2))
    wait_bytes(obuf, rsem.at[7])
    for half in range(2):
        result = obuf[8 * half].astype(f32)
        for k in range(1, 8):
            result = result + obuf[8 * half + k].astype(f32)
        out_ref[16 * half : 16 * half + 16, :] = result.astype(bf16)

    wait_bytes(qbuf.at[pl.ds(0, 31)], ssem.at[0])
    for copy in swap:
        copy.wait_send()
    tail_copy.wait_send()
    for copy in sends:
        copy.wait_send()
    wait_bytes(wbuf.at[pl.ds(0, 7)], ssem.at[4])
    wait_bytes(rbuf.at[pl.ds(0, 15)], ssem.at[6])
    wait_bytes(obuf.at[pl.ds(0, 15)], ssem.at[7])

    @pl.when(lax.div(y, 2) != c)
    def _():
        wait_bytes(rbuf.at[15], ssem.at[6])

    @pl.when(lax.div(x, 2) != c)
    def _():
        wait_bytes(obuf.at[15], ssem.at[7])


def on_device(*args):
    any_spec = pl.BlockSpec(memory_space=pl.ANY)
    smem = pl.BlockSpec(memory_space=pltpu.SMEM)
    specs = [any_spec] * 10
    specs[3] = specs[6] = smem
    return pl.pallas_call(
        kernel,
        out_shape=jax.ShapeDtypeStruct((32, 512), bf16),
        in_specs=specs,
        out_specs=pl.BlockSpec(memory_space=pltpu.VMEM),
        scratch_shapes=[
            pltpu.VMEM((2, 32, 128), bf16),
            pltpu.VMEM((4, 16, 128), bf16),
            pltpu.VMEM((32, 2, 16, 128), bf16),
            pltpu.VMEM((2, 2, 256, 128), bf16),
            pltpu.VMEM((2, 2, 256, 128), bf16),
            pltpu.VMEM((2, 2, 128, 256), bf16),
            pltpu.VMEM((4, 256, 128), bf16),
            pltpu.VMEM((4, 256, 128), bf16),
            pltpu.VMEM((2, 4, 128), bf16),
            pltpu.VMEM((2, 4, 128), bf16),
            pltpu.VMEM((8, 128), f32),
            pltpu.VMEM((2, 8, 128), f32),
            pltpu.VMEM((4, 128, 128), bf16),
            pltpu.VMEM((2, 136, 128), f32),
            pltpu.VMEM((2, 2, 136, 128), f32),
            pltpu.VMEM((4, 2, 2, 80, 128), bf16),
            pltpu.VMEM((16, 80, 128), bf16),
            pltpu.VMEM((16, 16, 512), bf16),
            pltpu.VMEM((8, 64, 512), bf16),
            pltpu.VMEM((16, 16, 512), bf16),
            pltpu.VMEM((16, 16, 512), bf16),
            pltpu.SemaphoreType.DMA((7,)),
            pltpu.SemaphoreType.DMA((8,)),
            pltpu.SemaphoreType.DMA((8,)),
            pltpu.SemaphoreType.DMA((16,)),
            pltpu.SemaphoreType.DMA((16,)),
        ],
        compiler_params=pltpu.CompilerParams(
            collective_id=0, has_side_effects=True, vmem_limit_bytes=32 * 1024 * 1024
        ),
        name="attend",
    )(*args)


def solution(mesh):
    placed = (
        P("prompt", "seq", None, None, None),
        P("prompt", None, "seq", None),
        P("prompt", None, "seq", None),
        P("prompt", None, "seq"),
        P("prompt", "seq", None, None, None),
        P("prompt", "seq", None, None, None),
        P("prompt", "seq"),
        P("prompt", "seq", None, None, None),
        P("prompt", "seq", None, None, None),
        P("seq", "prompt"),
    )
    return jax.shard_map(
        on_device, mesh=mesh, in_specs=placed, out_specs=P("seq", "prompt"), check_vma=False
    )
```

```python
import functools
import math

import jax
import jax.numpy as jnp
from jax import lax
from jax.experimental import pallas as pl
from jax.experimental.pallas import tpu as pltpu
from jax.sharding import PartitionSpec as P

MESH = pl.DeviceIdType.MESH
bf16 = jnp.bfloat16
f32 = jnp.float32
NEGATIVE = -1e30

NP = 16
NS = 32
SCALE = 1.0 / math.sqrt(128)
DIRECT = (8, 5, -5, 2, -2, 1, -1)
HOPS = sorted(
    ((dy, dx) for dy in range(4) for dx in range(4)),
    key=lambda t: -(min(t[0], 4 - t[0]) + min(t[1], 4 - t[1])),
)
NT = (((1,), (1,)), ((), ()))
TN = (((0,), (0,)), ((), ()))


def dot(a, b, dims=(((1,), (0,)), ((), ()))):
    return lax.dot_general(a, b, dims, preferred_element_type=f32)


def iota(shape, axis):
    return lax.broadcasted_iota(jnp.int32, shape, axis)


def kernel(
    q_ref, k_ref, v_ref, kept_hbm, sk_ref, sv_ref, len_hbm, dk_ref, dv_ref, w_ref,
    out_ref,
    qv, qsend, qbuf, kbuf, vbuf, vt, skv, svv, dkv, dvv, flag_out, flag, qpl,
    tail_out, tail, part, rbuf, laid_ref, zbuf, wbuf, psend, obuf,
    kept_ref, len_ref, lsem, ssem, rsem, zssem, zrsem,
):
    p, s = lax.axis_index("prompt"), lax.axis_index("seq")
    y, i = lax.div(s, 8), lax.rem(s, 8)
    x, c = lax.div(i, 2), lax.rem(s, 2)
    chip, other = lax.div(s, 2), 1 - c
    sib = s + 1 - 2 * c

    def at(plane, seq):
        return {"prompt": plane, "seq": seq}

    def zoff(o):
        return lax.rem(p + o + NP, NP)

    def remote(src, dst, send, recv, plane, seq):
        return pltpu.make_async_remote_copy(
            src, dst, send, recv, device_id=at(plane, seq), device_id_type=MESH
        )

    def wait_bytes(ref, sem):
        pltpu.make_async_copy(ref, ref, sem).wait()

    def send_or_keep(src, dst, n, seq):
        own = seq == s

        @pl.when(own)
        def _():
            pltpu.make_async_copy(src, dst, rsem.at[n]).start()

        @pl.when(jnp.logical_not(own))
        def _():
            remote(src, dst, ssem.at[n], rsem.at[n], p, seq).start()

    local = [
        pltpu.make_async_copy(q_ref.at[0, 0], qv, lsem.at[0]),
        pltpu.make_async_copy(sk_ref.at[0, 0], skv, lsem.at[1]),
        pltpu.make_async_copy(dk_ref.at[0, 0], dkv, lsem.at[2]),
        pltpu.make_async_copy(sv_ref.at[0, 0], svv, lsem.at[3]),
        pltpu.make_async_copy(dv_ref.at[0, 0], dvv, lsem.at[4]),
        pltpu.make_async_copy(k_ref.at[0, pl.ds(2 * c, 2)], kbuf.at[c], lsem.at[5]),
        pltpu.make_async_copy(v_ref.at[0, pl.ds(2 * c, 2)], vbuf.at[c], lsem.at[6]),
        pltpu.make_async_copy(kept_hbm, kept_ref, lsem.at[7]),
        pltpu.make_async_copy(len_hbm, len_ref, lsem.at[8]),
    ]
    for copy in local:
        copy.start()

    barrier = pltpu.get_barrier_semaphore()

    def greet(k, carry):
        pl.semaphore_signal(
            barrier, inc=1, device_id=at(p, lax.rem(s + k, NS)), device_id_type=MESH
        )
        return carry

    lax.fori_loop(1, NS, greet, 0)
    for o in DIRECT:
        for seq in (s, sib):
            pl.semaphore_signal(barrier, inc=1, device_id=at(zoff(o), seq), device_id_type=MESH)

    local[0].wait()
    heads = qv[...].astype(f32).reshape(2, 4, 8, 128)
    for h in range(4):
        rows = heads[:, h].reshape(16, 128).astype(bf16)
        qsend[h] = rows
    row8 = iota((8, 128), 0)

    def flags(core):
        first = kept_ref[0, 0, 2 * core].astype(f32)
        second = kept_ref[0, 0, 2 * core + 1].astype(f32)
        return jnp.where(row8 == 0, first, second)

    local[7].wait()
    flag[c] = flags(c)
    flag_out[...] = flags(other)

    pl.semaphore_wait(barrier, NS - 1 + 2 * len(DIRECT))

    for dy, dx in HOPS:
        base = lax.rem(y + dy, 4) * 8 + lax.rem(x + dx, 4) * 2
        for core in range(2):
            if (dy, dx) != (0, 0):
                remote(
                    qsend.at[pl.ds(2 * core, 2)], qbuf.at[s], ssem.at[0], rsem.at[0], p, base + core
                ).start()
    remote(qsend.at[pl.ds(2 * other, 2)], qbuf.at[s], ssem.at[0], rsem.at[0], p, sib).start()
    pltpu.make_async_copy(qsend.at[pl.ds(2 * c, 2)], qbuf.at[s], rsem.at[0]).start()
    swap = [
        remote(k_ref.at[0, pl.ds(2 * other, 2)], kbuf.at[c], ssem.at[1], rsem.at[1], p, sib),
        remote(v_ref.at[0, pl.ds(2 * other, 2)], vbuf.at[c], ssem.at[2], rsem.at[2], p, sib),
        remote(flag_out, flag.at[c], ssem.at[3], rsem.at[3], p, sib),
    ]
    for copy in swap:
        copy.start()
    for dx in (2, 1, 3):
        remote(
            w_ref, wbuf.at[c, :, x], ssem.at[4], rsem.at[4], p, y * 8 + lax.rem(x + dx, 4) * 2 + c
        ).start()
    pltpu.make_async_copy(w_ref, wbuf.at[c, :, x], rsem.at[4]).start()

    lane = iota((1, 128), 1)
    qpl[...] = jnp.zeros((4, 128, 128), bf16)
    for h in range(4):
        qpl[h, pl.ds(pl.multiple_of(16 * i, 16), 16), :] = qsend[h]
    for copy in local[1:5] + local[8:]:
        copy.wait()
    placed = qpl[...].reshape(512, 128)
    fresh = [dot(dkv[u], placed, NT) * SCALE for u in range(2)]
    later_step = lax.rem(lax.div(lane, 8), 2) == 1
    key_mask = iota((256, 128), 0) < len_ref[0, 0]
    row16 = iota((16, 128), 0)
    for h in range(4):
        scores = dot(skv[h], qpl[h], NT) * SCALE
        scores = jnp.where(key_mask, scores, NEGATIVE)
        f0 = fresh[0][h : h + 1, 128 * h : 128 * h + 128]
        f1 = jnp.where(later_step, fresh[1][h : h + 1, 128 * h : 128 * h + 128], NEGATIVE)
        top = jnp.maximum(jnp.max(scores, axis=0, keepdims=True), jnp.maximum(f0, f1))
        e = jnp.where(key_mask, jnp.exp(scores - top), 0.0)
        e0, e1 = jnp.exp(f0 - top), jnp.where(later_step, jnp.exp(f1 - top), 0.0)
        total = jnp.sum(e, axis=0, keepdims=True) + e0 + e1
        value0 = dvv[0].astype(f32)[h : h + 1]
        value1 = dvv[1].astype(f32)[h : h + 1]
        values = jnp.where(row16 == 0, value0, jnp.where(row16 == 1, value1, 0.0)).astype(bf16)
        weights = jnp.where(row16 == 0, e0, jnp.where(row16 == 1, e1, 0.0)).astype(bf16)
        o = dot(svv[h], e.astype(bf16), TN) + dot(values, weights, TN)
        stats = jnp.where(row8 == 0, top, total)
        core, j = h // 2, h % 2

        @pl.when(c == core)
        def _():
            tail[c, j, :128] = o
            tail[c, j, 128:] = stats

        @pl.when(c != core)
        def _():
            tail_out[j, :128] = o
            tail_out[j, 128:] = stats

    tail_copy = remote(tail_out, tail.at[c], ssem.at[5], rsem.at[5], p, sib)
    tail_copy.start()

    local[5].wait()
    local[6].wait()
    for n in (1, 2, 3):
        swap[n - 1].wait_recv()
    for j in range(2):
        for core in range(2):
            vt[j, core] = jnp.transpose(vbuf[core, j])
    tail_copy.wait_recv()

    wait_bytes(qbuf, rsem.at[0])
    def partial(kk, j):
        chunk = lax.rem(y + kk, 4)
        rows = qbuf[pl.ds(8 * chunk, 8), j].reshape(128, 128)
        tops, sums, outs = [], [], []
        for core in range(2):
            scores = dot(kbuf[core, j], rows, NT) * SCALE
            for slot in range(2):
                block = scores[128 * slot : 128 * slot + 128]
                block_max = jnp.max(block, axis=0, keepdims=True)
                e = jnp.exp(block - block_max)
                sums.append(jnp.sum(e, axis=0, keepdims=True))
                outs.append(dot(vt[j, core, :, 128 * slot : 128 * slot + 128], e.astype(bf16)))
                if slot == 1:
                    live = flag[core, j : j + 1, :] > 1.5
                    block_max = jnp.where(live, block_max, NEGATIVE)
                tops.append(block_max)
        if kk == 0:
            for core in range(2):
                mine = lax.div(lane, 16) == 2 * x + core
                tops.append(jnp.where(mine, tail[core, j, 128:129], NEGATIVE))
                sums.append(tail[core, j, 129:130])
                outs.append(tail[core, j, :128])
        top = functools.reduce(jnp.maximum, tops).astype(bf16).astype(f32)
        total, summed = 0.0, 0.0
        for m, t, o in zip(tops, sums, outs):
            factor = jnp.exp(m - top)
            total = total + factor * t
            summed = summed + factor * o
        high = total.astype(bf16).astype(f32)
        stats = jnp.where(row16 == 0, top, jnp.where(row16 == 1, high, total - high))
        stats = stats.astype(bf16)
        summed = summed.astype(bf16)
        for half in range(2):
            part[kk, j, half, :64] = summed[64 * half : 64 * half + 64]
            part[kk, j, half, 64:] = stats

    for group in ((0, 1), (2, 3)):
        for kk in group:
            for j in range(2):
                partial(kk, j)
        for kk in group:
            chunk = lax.rem(y + kk, 4)
            for j in range(2):
                for half in range(2):
                    send_or_keep(
                        part.at[kk, j, half], rbuf.at[chip], 6, (2 * c + j) * 8 + chunk * 2 + half
                    )

    wait_bytes(rbuf, rsem.at[6])
    tops = [rbuf[k, 64:80].astype(f32) for k in range(16)]
    top = functools.reduce(jnp.maximum, [t[0:1] for t in tops])
    total, summed = 0.0, 0.0
    for k in range(16):
        factor = jnp.exp(tops[k][0:1] - top)
        total = total + factor * (tops[k][1:2] + tops[k][2:3])
        summed = summed + factor * rbuf[k, :64].astype(f32)
    head_out = (summed / total).astype(bf16)
    blank = jnp.zeros_like(head_out)
    stacked = jnp.concatenate(
        [jnp.concatenate([head_out, blank], axis=1), jnp.concatenate([blank, head_out], axis=1)],
        axis=0,
    )
    a, b = iota((64, 256), 0), iota((64, 256), 1)
    place = 2 * lax.div(a, 16) + lax.div(b, 128)
    wanted = lax.rem(a, 16) * 8 + 2 * lax.rem(place, 4) + lax.div(place, 4)
    pick = jnp.where(lax.rem(b, 128) == wanted, 1.0, 0.0).astype(bf16)
    laid = dot(pick, stacked, NT).astype(bf16)
    for g in range(4):
        laid_ref[:, 128 * g : 128 * g + 128] = laid[16 * g : 16 * g + 16]

    parity = lax.rem(p, 2)
    own_slot = zbuf.at[lax.div(p, 2)]
    for o in DIRECT:
        remote(
            laid_ref, own_slot.at[c], zssem.at[0], zrsem.at[lax.div(p, 2)], zoff(o), s - c + parity
        ).start()

    @pl.when(c == parity)
    def _():
        pltpu.make_async_copy(laid_ref, own_slot.at[c], zrsem.at[lax.div(p, 2)]).start()

    @pl.when(c != parity)
    def _():
        remote(laid_ref, own_slot.at[c], zssem.at[1], zrsem.at[lax.div(p, 2)], p, sib).start()

    wait_bytes(wbuf.at[c], rsem.at[4])
    remote(wbuf.at[c], wbuf.at[c], ssem.at[7], rsem.at[8], p, sib).start()

    def zwait(q):
        wait_bytes(zbuf.at[lax.div(q, 2)], zrsem.at[lax.div(q, 2)])

    def relay(source, onward):
        for sign in (1, -1):
            q = zoff(-sign * source)
            zwait(q)
            slot = lax.div(q, 2)
            for o in onward:
                remote(
                    zbuf.at[slot], zbuf.at[slot], zssem.at[2], zrsem.at[slot], zoff(sign * o), s
                ).start()

    odd = lax.rem(p + c, 2)

    @pl.when(odd == 1)
    def _():
        relay(5, (2, 1, -1))

    @pl.when(odd == 0)
    def _():
        relay(2, (1,))

    wait_bytes(wbuf.at[other], rsem.at[8])
    mine = lax.rem(x, 2) * 4 + y
    near = (5 * odd + 2 * (1 - odd), -5 * odd - 2 * (1 - odd), odd, 8 - 9 * odd)
    far = (3 * odd + 4 * (1 - odd), -3 * odd - 4 * (1 - odd), 7 * odd + 6 * (1 - odd), -7 * odd - 6 * (1 - odd))
    for n, group in enumerate((near, far)):
        planes = [zoff(o) for o in group]
        for q in planes[2:] if n == 0 else planes:
            zwait(q)
        terms = 0.0
        for half in range(2):
            rows = jnp.concatenate([zbuf[lax.div(q, 2), half] for q in planes], axis=0)
            for core in range(2):
                terms = terms + dot(
                    rows[:, 256 * core : 256 * core + 256], wbuf[core, half].reshape(256, 512)
                )
        psend[4 * n : 4 * n + 4] = terms.astype(bf16).reshape(4, 16, 512)
        for k, q in enumerate(planes):
            send_or_keep(psend.at[4 * n + k], obuf.at[mine], 9, 2 * q + lax.div(x, 2))
    wait_bytes(obuf, rsem.at[9])
    for half in range(2):
        result = obuf[4 * half].astype(f32)
        for k in range(1, 4):
            result = result + obuf[4 * half + k].astype(f32)
        out_ref[16 * half : 16 * half + 16, :] = result.astype(bf16)

    wait_bytes(qbuf.at[pl.ds(0, 31)], ssem.at[0])
    for copy in swap:
        copy.wait_send()
    tail_copy.wait_send()
    wait_bytes(wbuf.at[0, :, pl.ds(0, 3)], ssem.at[4])
    wait_bytes(rbuf.at[pl.ds(0, 15)], ssem.at[6])

    @pl.when(lax.div(y, 2) != c)
    def _():
        wait_bytes(rbuf.at[15], ssem.at[6])

    wait_bytes(wbuf.at[0], ssem.at[7])
    wait_bytes(zbuf.at[pl.ds(0, len(DIRECT)), 0], zssem.at[0])

    @pl.when(c != parity)
    def _():
        wait_bytes(laid_ref, zssem.at[1])

    wait_bytes(zbuf.at[pl.ds(0, 2)], zssem.at[2])

    @pl.when(odd == 1)
    def _():
        wait_bytes(zbuf.at[pl.ds(0, 4)], zssem.at[2])

    wait_bytes(obuf.at[pl.ds(0, 7)], ssem.at[9])

    @pl.when(x != 3 * c)
    def _():
        wait_bytes(obuf.at[7], ssem.at[9])


def on_device(*args):
    args = list(args)
    args[3] = jnp.transpose(args[3], (0, 2, 1))
    args[9] = args[9].reshape(2, 64, 512)
    return pl.pallas_call(
        kernel,
        out_shape=jax.ShapeDtypeStruct((32, 512), bf16),
        in_specs=[pl.BlockSpec(memory_space=pltpu.HBM)] * 10,
        out_specs=pl.BlockSpec(memory_space=pltpu.VMEM),
        scratch_shapes=[
            pltpu.VMEM((2, 32, 128), bf16),
            pltpu.VMEM((4, 16, 128), bf16),
            pltpu.VMEM((32, 2, 16, 128), bf16),
            pltpu.VMEM((2, 2, 256, 128), bf16),
            pltpu.VMEM((2, 2, 256, 128), bf16),
            pltpu.VMEM((2, 2, 128, 256), bf16),
            pltpu.VMEM((4, 256, 128), bf16),
            pltpu.VMEM((4, 256, 128), bf16),
            pltpu.VMEM((2, 4, 128), bf16),
            pltpu.VMEM((2, 4, 128), bf16),
            pltpu.VMEM((8, 128), f32),
            pltpu.VMEM((2, 8, 128), f32),
            pltpu.VMEM((4, 128, 128), bf16),
            pltpu.VMEM((2, 136, 128), f32),
            pltpu.VMEM((2, 2, 136, 128), f32),
            pltpu.VMEM((4, 2, 2, 80, 128), bf16),
            pltpu.VMEM((16, 80, 128), bf16),
            pltpu.VMEM((16, 512), bf16),
            pltpu.VMEM((8, 2, 16, 512), bf16),
            pltpu.VMEM((2, 2, 4, 64, 512), bf16),
            pltpu.VMEM((8, 16, 512), bf16),
            pltpu.VMEM((8, 16, 512), bf16),
            pltpu.SMEM((1, 1, 4), jnp.int32),
            pltpu.SMEM((1, 1), jnp.int32),
            pltpu.SemaphoreType.DMA((9,)),
            pltpu.SemaphoreType.DMA((10,)),
            pltpu.SemaphoreType.DMA((10,)),
            pltpu.SemaphoreType.DMA((3,)),
            pltpu.SemaphoreType.DMA((8,)),
        ],
        compiler_params=pltpu.CompilerParams(
            collective_id=0, has_side_effects=True, vmem_limit_bytes=56 * 1024 * 1024
        ),
        name="attend",
    )(*args)


def solution(mesh):
    placed = (
        P("prompt", "seq", None, None, None),
        P("prompt", None, "seq", None),
        P("prompt", None, "seq", None),
        P("prompt", None, "seq"),
        P("prompt", "seq", None, None, None),
        P("prompt", "seq", None, None, None),
        P("prompt", "seq"),
        P("prompt", "seq", None, None, None),
        P("prompt", "seq", None, None, None),
        P("seq", "prompt"),
    )
    return jax.shard_map(
        on_device, mesh=mesh, in_specs=placed, out_specs=P("seq", "prompt"), check_vma=False
    )
```

```python
import functools
import math

import jax
import jax.numpy as jnp
from jax import lax
from jax.experimental import pallas as pl
from jax.experimental.pallas import tpu as pltpu
from jax.sharding import PartitionSpec as P

MESH = pl.DeviceIdType.MESH
bf16 = jnp.bfloat16
f32 = jnp.float32
NEGATIVE = -1e30

NP = 16
NS = 32
SCALE = 1.0 / math.sqrt(128)
DIRECT = (8, 5, -5, 2, -2, 1, -1)
HOPS = sorted(
    ((dy, dx) for dy in range(4) for dx in range(4)),
    key=lambda t: -(min(t[0], 4 - t[0]) + min(t[1], 4 - t[1])),
)
NT = (((1,), (1,)), ((), ()))
TN = (((0,), (0,)), ((), ()))


def dot(a, b, dims=(((1,), (0,)), ((), ()))):
    return lax.dot_general(a, b, dims, preferred_element_type=f32)


def iota(shape, axis):
    return lax.broadcasted_iota(jnp.int32, shape, axis)


def kernel(
    q_ref, k_ref, v_ref, kept_hbm, sk_ref, sv_ref, len_hbm, dk_ref, dv_ref, w_ref,
    obuf,
    qv, qsend, qbuf, kbuf, vbuf, vt, skv, svv, dkv, dvv, flag_out, flag, qpl,
    tail_out, tail, part, rbuf, laid_ref, zbuf, wbuf, psend,
    kept_ref, len_ref, lsem, ssem, rsem, zssem, zrsem, qrsem, known,
):
    p, s = lax.axis_index("prompt"), lax.axis_index("seq")
    y, i = lax.div(s, 8), lax.rem(s, 8)
    x, c = lax.div(i, 2), lax.rem(s, 2)
    chip, other = lax.div(s, 2), 1 - c
    sib = s + 1 - 2 * c

    def at(plane, seq):
        return {"prompt": plane, "seq": seq}

    def zoff(o):
        return lax.rem(p + o + NP, NP)

    def remote(src, dst, send, recv, plane, seq):
        return pltpu.make_async_remote_copy(
            src, dst, send, recv, device_id=at(plane, seq), device_id_type=MESH
        )

    def wait_bytes(ref, sem):
        pltpu.make_async_copy(ref, ref, sem).wait()

    def send_or_keep(src, dst, n, seq):
        own = seq == s

        @pl.when(own)
        def _():
            pltpu.make_async_copy(src, dst, rsem.at[n]).start()

        @pl.when(jnp.logical_not(own))
        def _():
            remote(src, dst, ssem.at[n], rsem.at[n], p, seq).start()

    local = [
        pltpu.make_async_copy(q_ref.at[0, 0], qv, lsem.at[0]),
        pltpu.make_async_copy(sk_ref.at[0, 0], skv, lsem.at[1]),
        pltpu.make_async_copy(dk_ref.at[0, 0], dkv, lsem.at[2]),
        pltpu.make_async_copy(sv_ref.at[0, 0], svv, lsem.at[3]),
        pltpu.make_async_copy(dv_ref.at[0, 0], dvv, lsem.at[4]),
        pltpu.make_async_copy(k_ref.at[0, pl.ds(2 * c, 2)], kbuf.at[c], lsem.at[5]),
        pltpu.make_async_copy(v_ref.at[0, pl.ds(2 * c, 2)], vbuf.at[c], lsem.at[6]),
        pltpu.make_async_copy(kept_hbm, kept_ref, lsem.at[7]),
        pltpu.make_async_copy(len_hbm, len_ref, lsem.at[8]),
    ]
    for copy in local:
        copy.start()

    barrier = pltpu.get_barrier_semaphore()

    def greet(k, carry):
        pl.semaphore_signal(
            barrier, inc=1, device_id=at(p, lax.rem(s + k, NS)), device_id_type=MESH
        )
        return carry

    lax.fori_loop(1, NS, greet, 0)
    for o in (2, -2, 1, -1):
        for seq in (s, sib):
            pl.semaphore_signal(barrier, inc=1, device_id=at(zoff(o), seq), device_id_type=MESH)

    local[0].wait()
    heads = qv[...].astype(f32).reshape(2, 4, 8, 128)
    for h in range(4):
        rows = heads[:, h].reshape(16, 128).astype(bf16)
        qsend[h] = rows
    row8 = iota((8, 128), 0)

    def flags(core):
        first = kept_ref[0, 0, 2 * core].astype(f32)
        second = kept_ref[0, 0, 2 * core + 1].astype(f32)
        return jnp.where(row8 == 0, first, second)

    local[7].wait()
    flag[c] = flags(c)
    flag_out[...] = flags(other)

    lane = iota((1, 128), 1)
    qpl[...] = jnp.zeros((4, 128, 128), bf16)
    for h in range(4):
        qpl[h, pl.ds(pl.multiple_of(16 * i, 16), 16), :] = qsend[h]
    for copy in local[1:5] + local[8:]:
        copy.wait()
    placed = qpl[...].reshape(512, 128)
    fresh = [dot(dkv[u], placed, NT) * SCALE for u in range(2)]
    later_step = lax.rem(lax.div(lane, 8), 2) == 1
    key_mask = iota((256, 128), 0) < len_ref[0, 0]
    row16 = iota((16, 128), 0)
    for h in range(4):
        scores = dot(skv[h], qpl[h], NT) * SCALE
        scores = jnp.where(key_mask, scores, NEGATIVE)
        f0 = fresh[0][h : h + 1, 128 * h : 128 * h + 128]
        f1 = jnp.where(later_step, fresh[1][h : h + 1, 128 * h : 128 * h + 128], NEGATIVE)
        top = jnp.maximum(jnp.max(scores, axis=0, keepdims=True), jnp.maximum(f0, f1))
        e = jnp.where(key_mask, jnp.exp(scores - top), 0.0)
        e0, e1 = jnp.exp(f0 - top), jnp.where(later_step, jnp.exp(f1 - top), 0.0)
        total = jnp.sum(e, axis=0, keepdims=True) + e0 + e1
        value0 = dvv[0].astype(f32)[h : h + 1]
        value1 = dvv[1].astype(f32)[h : h + 1]
        values = jnp.where(row16 == 0, value0, jnp.where(row16 == 1, value1, 0.0)).astype(bf16)
        weights = jnp.where(row16 == 0, e0, jnp.where(row16 == 1, e1, 0.0)).astype(bf16)
        o = dot(svv[h], e.astype(bf16), TN) + dot(values, weights, TN)
        stats = jnp.where(row8 == 0, top, total)
        core, j = h // 2, h % 2

        @pl.when(c == core)
        def _():
            tail[c, j, :128] = o
            tail[c, j, 128:] = stats

        @pl.when(c != core)
        def _():
            tail_out[j, :128] = o
            tail_out[j, 128:] = stats

    local[5].wait()
    local[6].wait()
    for j in range(2):
        vt[j, c] = jnp.transpose(vbuf[c, j])

    pl.semaphore_wait(barrier, NS - 1 + 8)

    def spread(n, o):
        for sign in (1, -1):
            pl.semaphore_signal(
                known.at[n], inc=1, device_id=at(zoff(sign * o), s), device_id_type=MESH
            )

    spread(0, 2)

    swap = [
        remote(k_ref.at[0, pl.ds(2 * other, 2)], kbuf.at[c], ssem.at[1], rsem.at[1], p, sib),
        remote(v_ref.at[0, pl.ds(2 * other, 2)], vbuf.at[c], ssem.at[2], rsem.at[2], p, sib),
        remote(flag_out, flag.at[c], ssem.at[3], rsem.at[3], p, sib),
    ]
    for copy in swap:
        copy.start()
    tail_copy = remote(tail_out, tail.at[c], ssem.at[5], rsem.at[5], p, sib)
    tail_copy.start()


    for dy, dx in reversed(HOPS):
        base = lax.rem(y + dy, 4) * 8 + lax.rem(x + dx, 4) * 2
        for core in range(2):
            if (dy, dx) != (0, 0):
                remote(
                    qsend.at[pl.ds(2 * core, 2)], qbuf.at[s], ssem.at[0], qrsem.at[y], p, base + core
                ).start()
    remote(qsend.at[pl.ds(2 * other, 2)], qbuf.at[s], ssem.at[0], qrsem.at[y], p, sib).start()
    pltpu.make_async_copy(qsend.at[pl.ds(2 * c, 2)], qbuf.at[s], qrsem.at[y]).start()
    for n in (1, 2, 3):
        swap[n - 1].wait_recv()
    for j in range(2):
        vt[j, other] = jnp.transpose(vbuf[other, j])
    tail_copy.wait_recv()

    def partial(kk, j):
        chunk = lax.rem(y + kk, 4)
        rows = qbuf[pl.ds(8 * chunk, 8), j].reshape(128, 128)
        tops, sums, outs = [], [], []
        for core in range(2):
            scores = dot(kbuf[core, j], rows, NT) * SCALE
            for slot in range(2):
                block = scores[128 * slot : 128 * slot + 128]
                block_max = jnp.max(block, axis=0, keepdims=True)
                e = jnp.exp(block - block_max)
                sums.append(jnp.sum(e, axis=0, keepdims=True))
                outs.append(dot(vt[j, core, :, 128 * slot : 128 * slot + 128], e.astype(bf16)))
                if slot == 1:
                    live = flag[core, j : j + 1, :] > 1.5
                    block_max = jnp.where(live, block_max, NEGATIVE)
                tops.append(block_max)
        if kk == 0:
            for core in range(2):
                mine = lax.div(lane, 16) == 2 * x + core
                tops.append(jnp.where(mine, tail[core, j, 128:129], NEGATIVE))
                sums.append(tail[core, j, 129:130])
                outs.append(tail[core, j, :128])
        top = functools.reduce(jnp.maximum, tops).astype(bf16).astype(f32)
        total, summed = 0.0, 0.0
        for m, t, o in zip(tops, sums, outs):
            factor = jnp.exp(m - top)
            total = total + factor * t
            summed = summed + factor * o
        high = total.astype(bf16).astype(f32)
        stats = jnp.where(row16 == 0, top, jnp.where(row16 == 1, high, total - high))
        stats = stats.astype(bf16)
        summed = summed.astype(bf16)
        for half in range(2):
            part[kk, j, half, :64] = summed[64 * half : 64 * half + 64]
            part[kk, j, half, 64:] = stats

    for kk in (0, 1, 3, 2):
        chunk = lax.rem(y + kk, 4)
        wait_bytes(qbuf.at[pl.ds(8 * chunk, 8)], qrsem.at[chunk])
        for j in range(2):
            partial(kk, j)
        for j in range(2):
            for half in range(2):
                send_or_keep(
                    part.at[kk, j, half], rbuf.at[chip], 6, (2 * c + j) * 8 + chunk * 2 + half
                )

    pl.semaphore_wait(known.at[0], 2)
    spread(1, 4)

    wait_bytes(rbuf, rsem.at[6])
    for dx in (2, 1, 3):
        remote(
            w_ref, wbuf.at[c, :, x], ssem.at[4], rsem.at[4], p, y * 8 + lax.rem(x + dx, 4) * 2 + c
        ).start()
    pltpu.make_async_copy(w_ref, wbuf.at[c, :, x], rsem.at[4]).start()

    tops = [rbuf[k, 64:80].astype(f32) for k in range(16)]
    top = functools.reduce(jnp.maximum, [t[0:1] for t in tops])
    total, summed = 0.0, 0.0
    for k in range(16):
        factor = jnp.exp(tops[k][0:1] - top)
        total = total + factor * (tops[k][1:2] + tops[k][2:3])
        summed = summed + factor * rbuf[k, :64].astype(f32)
    head_out = (summed / total).astype(bf16)
    blank = jnp.zeros_like(head_out)
    stacked = jnp.concatenate(
        [jnp.concatenate([head_out, blank], axis=1), jnp.concatenate([blank, head_out], axis=1)],
        axis=0,
    )
    a, b = iota((64, 256), 0), iota((64, 256), 1)
    place = 2 * lax.div(a, 16) + lax.div(b, 128)
    wanted = lax.rem(a, 16) * 8 + 2 * lax.rem(place, 4) + lax.div(place, 4)
    pick = jnp.where(lax.rem(b, 128) == wanted, 1.0, 0.0).astype(bf16)
    laid = dot(pick, stacked, NT).astype(bf16)
    for g in range(4):
        laid_ref[:, 128 * g : 128 * g + 128] = laid[16 * g : 16 * g + 16]

    pl.semaphore_wait(known.at[1], 2)
    parity = lax.rem(p, 2)
    own_slot = zbuf.at[lax.div(p, 2)]
    for o in DIRECT:
        remote(
            laid_ref, own_slot.at[c], zssem.at[0], zrsem.at[lax.div(p, 2)], zoff(o), s - c + parity
        ).start()

    @pl.when(c == parity)
    def _():
        pltpu.make_async_copy(laid_ref, own_slot.at[c], zrsem.at[lax.div(p, 2)]).start()

    @pl.when(c != parity)
    def _():
        remote(laid_ref, own_slot.at[c], zssem.at[1], zrsem.at[lax.div(p, 2)], p, sib).start()

    def zwait(q):
        wait_bytes(zbuf.at[lax.div(q, 2)], zrsem.at[lax.div(q, 2)])

    def relay(source, onward):
        for sign in (1, -1):
            q = zoff(-sign * source)
            zwait(q)
            slot = lax.div(q, 2)
            for o in onward:
                remote(
                    zbuf.at[slot], zbuf.at[slot], zssem.at[2], zrsem.at[slot], zoff(sign * o), s
                ).start()

    odd = lax.rem(p + c, 2)

    @pl.when(odd == 1)
    def _():
        relay(5, (2, 1, -1))

    @pl.when(odd == 0)
    def _():
        relay(2, (1,))

    wait_bytes(wbuf.at[c], rsem.at[4])
    remote(wbuf.at[c], wbuf.at[c], ssem.at[7], rsem.at[8], p, sib).start()

    wait_bytes(wbuf.at[other], rsem.at[8])
    mine = lax.rem(x, 2) * 4 + y
    near = (5 * odd + 2 * (1 - odd), -5 * odd - 2 * (1 - odd), odd, 8 - 9 * odd)
    far = (3 * odd + 4 * (1 - odd), -3 * odd - 4 * (1 - odd), 7 * odd + 6 * (1 - odd), -7 * odd - 6 * (1 - odd))
    for n, group in enumerate((near, far)):
        planes = [zoff(o) for o in group]
        for q in planes[2:] if n == 0 else planes:
            zwait(q)
        terms = 0.0
        for half in range(2):
            rows = jnp.concatenate([zbuf[lax.div(q, 2), half] for q in planes], axis=0)
            for core in range(2):
                terms = terms + dot(
                    rows[:, 256 * core : 256 * core + 256], wbuf[core, half].reshape(256, 512)
                )
        psend[4 * n : 4 * n + 4] = terms.astype(bf16).reshape(4, 16, 512)
        for k, q in enumerate(planes):
            send_or_keep(psend.at[4 * n + k], obuf.at[mine], 9, 2 * q + lax.div(x, 2))
    wait_bytes(obuf, rsem.at[9])
    wait_bytes(qbuf.at[pl.ds(0, 31)], ssem.at[0])
    for copy in swap:
        copy.wait_send()
    tail_copy.wait_send()
    wait_bytes(wbuf.at[0, :, pl.ds(0, 3)], ssem.at[4])
    wait_bytes(rbuf.at[pl.ds(0, 15)], ssem.at[6])

    @pl.when(lax.div(y, 2) != c)
    def _():
        wait_bytes(rbuf.at[15], ssem.at[6])

    wait_bytes(wbuf.at[0], ssem.at[7])
    wait_bytes(zbuf.at[pl.ds(0, len(DIRECT)), 0], zssem.at[0])

    @pl.when(c != parity)
    def _():
        wait_bytes(laid_ref, zssem.at[1])

    wait_bytes(zbuf.at[pl.ds(0, 2)], zssem.at[2])

    @pl.when(odd == 1)
    def _():
        wait_bytes(zbuf.at[pl.ds(0, 4)], zssem.at[2])

    wait_bytes(obuf.at[pl.ds(0, 7)], ssem.at[9])

    @pl.when(x != 3 * c)
    def _():
        wait_bytes(obuf.at[7], ssem.at[9])


def on_device(*args):
    args = list(args)
    args[3] = jnp.transpose(args[3], (0, 2, 1))
    args[9] = args[9].reshape(2, 64, 512)
    terms = pl.pallas_call(
        kernel,
        out_shape=jax.ShapeDtypeStruct((8, 16, 512), bf16),
        in_specs=[pl.BlockSpec(memory_space=pltpu.HBM)] * 10,
        out_specs=pl.BlockSpec(memory_space=pltpu.HBM),
        scratch_shapes=[
            pltpu.VMEM((2, 32, 128), bf16),
            pltpu.VMEM((4, 16, 128), bf16),
            pltpu.VMEM((32, 2, 16, 128), bf16),
            pltpu.VMEM((2, 2, 256, 128), bf16),
            pltpu.VMEM((2, 2, 256, 128), bf16),
            pltpu.VMEM((2, 2, 128, 256), bf16),
            pltpu.VMEM((4, 256, 128), bf16),
            pltpu.VMEM((4, 256, 128), bf16),
            pltpu.VMEM((2, 4, 128), bf16),
            pltpu.VMEM((2, 4, 128), bf16),
            pltpu.VMEM((8, 128), f32),
            pltpu.VMEM((2, 8, 128), f32),
            pltpu.VMEM((4, 128, 128), bf16),
            pltpu.VMEM((2, 136, 128), f32),
            pltpu.VMEM((2, 2, 136, 128), f32),
            pltpu.VMEM((4, 2, 2, 80, 128), bf16),
            pltpu.VMEM((16, 80, 128), bf16),
            pltpu.VMEM((16, 512), bf16),
            pltpu.VMEM((8, 2, 16, 512), bf16),
            pltpu.VMEM((2, 2, 4, 64, 512), bf16),
            pltpu.VMEM((8, 16, 512), bf16),
            pltpu.SMEM((1, 1, 4), jnp.int32),
            pltpu.SMEM((1, 1), jnp.int32),
            pltpu.SemaphoreType.DMA((9,)),
            pltpu.SemaphoreType.DMA((10,)),
            pltpu.SemaphoreType.DMA((10,)),
            pltpu.SemaphoreType.DMA((3,)),
            pltpu.SemaphoreType.DMA((8,)),
            pltpu.SemaphoreType.DMA((4,)),
            pltpu.SemaphoreType.REGULAR((2,)),
        ],
        compiler_params=pltpu.CompilerParams(
            collective_id=0, has_side_effects=True, vmem_limit_bytes=56 * 1024 * 1024
        ),
        name="attend",
    )(*args)
    terms = terms.reshape(2, 4, 16, 512).astype(f32)
    return jnp.sum(terms, axis=1).reshape(32, 512).astype(bf16)


def solution(mesh):
    placed = (
        P("prompt", "seq", None, None, None),
        P("prompt", None, "seq", None),
        P("prompt", None, "seq", None),
        P("prompt", None, "seq"),
        P("prompt", "seq", None, None, None),
        P("prompt", "seq", None, None, None),
        P("prompt", "seq"),
        P("prompt", "seq", None, None, None),
        P("prompt", "seq", None, None, None),
        P("seq", "prompt"),
    )
    return jax.shard_map(
        on_device, mesh=mesh, in_specs=placed, out_specs=P("seq", "prompt"), check_vma=False
    )
```

```python
import functools
import math

import jax
import jax.numpy as jnp
from jax import lax
from jax.experimental import pallas as pl
from jax.experimental.pallas import tpu as pltpu
from jax.sharding import PartitionSpec as P

MESH = pl.DeviceIdType.MESH
bf16 = jnp.bfloat16
f32 = jnp.float32
NEGATIVE = -1e30

NP = 16
NS = 32
SCALE = 1.0 / math.sqrt(128)
DIRECT = (5, -5, 8, 2, -2, 1, -1)
HOPS = sorted(
    ((dy, dx) for dy in range(4) for dx in range(4)),
    key=lambda t: -(min(t[0], 4 - t[0]) + min(t[1], 4 - t[1])),
)
NT = (((1,), (1,)), ((), ()))
TN = (((0,), (0,)), ((), ()))


def dot(a, b, dims=(((1,), (0,)), ((), ()))):
    return lax.dot_general(a, b, dims, preferred_element_type=f32)


def iota(shape, axis):
    return lax.broadcasted_iota(jnp.int32, shape, axis)


def kernel(
    q_ref, k_ref, v_ref, kept_hbm, sk_ref, sv_ref, len_hbm, dk_ref, dv_ref, w_ref,
    obuf,
    qv, qsend, qbuf, kbuf, vbuf, vt, skv, svv, dkv, dvv, flag_out, flag, qpl,
    tail_out, tail, part, rbuf, laid_ref, zbuf, wbuf, psend,
    kept_ref, len_ref, lsem, ssem, rsem, zssem, zrsem, qrsem, known,
):
    p, s = lax.axis_index("prompt"), lax.axis_index("seq")
    y, i = lax.div(s, 8), lax.rem(s, 8)
    x, c = lax.div(i, 2), lax.rem(s, 2)
    chip, other = lax.div(s, 2), 1 - c
    sib = s + 1 - 2 * c

    def at(plane, seq):
        return {"prompt": plane, "seq": seq}

    def zoff(o):
        return lax.rem(p + o + NP, NP)

    def remote(src, dst, send, recv, plane, seq):
        return pltpu.make_async_remote_copy(
            src, dst, send, recv, device_id=at(plane, seq), device_id_type=MESH
        )

    def wait_bytes(ref, sem):
        pltpu.make_async_copy(ref, ref, sem).wait()

    def send_or_keep(src, dst, n, seq):
        own = seq == s

        @pl.when(own)
        def _():
            pltpu.make_async_copy(src, dst, rsem.at[n]).start()

        @pl.when(jnp.logical_not(own))
        def _():
            remote(src, dst, ssem.at[n], rsem.at[n], p, seq).start()

    local = [
        pltpu.make_async_copy(q_ref.at[0, 0], qv, lsem.at[0]),
        pltpu.make_async_copy(sk_ref.at[0, 0], skv, lsem.at[1]),
        pltpu.make_async_copy(dk_ref.at[0, 0], dkv, lsem.at[2]),
        pltpu.make_async_copy(sv_ref.at[0, 0], svv, lsem.at[3]),
        pltpu.make_async_copy(dv_ref.at[0, 0], dvv, lsem.at[4]),
        pltpu.make_async_copy(k_ref.at[0, pl.ds(2 * c, 2)], kbuf.at[c], lsem.at[5]),
        pltpu.make_async_copy(v_ref.at[0, pl.ds(2 * c, 2)], vbuf.at[c], lsem.at[6]),
        pltpu.make_async_copy(kept_hbm, kept_ref, lsem.at[7]),
        pltpu.make_async_copy(len_hbm, len_ref, lsem.at[8]),
    ]
    for copy in local:
        copy.start()

    barrier = pltpu.get_barrier_semaphore()

    def greet(k, carry):
        pl.semaphore_signal(
            barrier, inc=1, device_id=at(p, lax.rem(s + k, NS)), device_id_type=MESH
        )
        return carry

    lax.fori_loop(1, NS, greet, 0)
    for o in (2, -2, 1, -1):
        for seq in (s, sib):
            pl.semaphore_signal(barrier, inc=1, device_id=at(zoff(o), seq), device_id_type=MESH)

    local[0].wait()
    heads = qv[...].astype(f32).reshape(2, 4, 8, 128)
    for h in range(4):
        rows = heads[:, h].reshape(16, 128).astype(bf16)
        qsend[h] = rows
    row8 = iota((8, 128), 0)

    def flags(core):
        first = kept_ref[0, 0, 2 * core].astype(f32)
        second = kept_ref[0, 0, 2 * core + 1].astype(f32)
        return jnp.where(row8 == 0, first, second)

    local[7].wait()
    flag[c] = flags(c)
    flag_out[...] = flags(other)

    lane = iota((1, 128), 1)
    qpl[...] = jnp.zeros((4, 128, 128), bf16)
    for h in range(4):
        qpl[h, pl.ds(pl.multiple_of(16 * i, 16), 16), :] = qsend[h]
    for copy in local[1:5] + local[8:]:
        copy.wait()
    placed = qpl[...].reshape(512, 128)
    fresh = [dot(dkv[u], placed, NT) * SCALE for u in range(2)]
    later_step = lax.rem(lax.div(lane, 8), 2) == 1
    key_mask = iota((256, 128), 0) < len_ref[0, 0]
    row16 = iota((16, 128), 0)
    for h in range(4):
        scores = dot(skv[h], qpl[h], NT) * SCALE
        scores = jnp.where(key_mask, scores, NEGATIVE)
        f0 = fresh[0][h : h + 1, 128 * h : 128 * h + 128]
        f1 = jnp.where(later_step, fresh[1][h : h + 1, 128 * h : 128 * h + 128], NEGATIVE)
        top = jnp.maximum(jnp.max(scores, axis=0, keepdims=True), jnp.maximum(f0, f1))
        e = jnp.where(key_mask, jnp.exp(scores - top), 0.0)
        e0, e1 = jnp.exp(f0 - top), jnp.where(later_step, jnp.exp(f1 - top), 0.0)
        total = jnp.sum(e, axis=0, keepdims=True) + e0 + e1
        value0 = dvv[0].astype(f32)[h : h + 1]
        value1 = dvv[1].astype(f32)[h : h + 1]
        values = jnp.where(row16 == 0, value0, jnp.where(row16 == 1, value1, 0.0)).astype(bf16)
        weights = jnp.where(row16 == 0, e0, jnp.where(row16 == 1, e1, 0.0)).astype(bf16)
        o = dot(svv[h], e.astype(bf16), TN) + dot(values, weights, TN)
        stats = jnp.where(row8 == 0, top, total)
        core, j = h // 2, h % 2

        @pl.when(c == core)
        def _():
            tail[c, j, :128] = o
            tail[c, j, 128:] = stats

        @pl.when(c != core)
        def _():
            tail_out[j, :128] = o
            tail_out[j, 128:] = stats

    local[5].wait()
    local[6].wait()
    for j in range(2):
        vt[j, c] = jnp.transpose(vbuf[c, j])

    pl.semaphore_wait(barrier, NS - 1 + 8)

    def spread(n, o):
        for sign in (1, -1):
            pl.semaphore_signal(
                known.at[n], inc=1, device_id=at(zoff(sign * o), s), device_id_type=MESH
            )

    spread(0, 2)

    swap = [
        remote(k_ref.at[0, pl.ds(2 * other, 2)], kbuf.at[c], ssem.at[1], rsem.at[1], p, sib),
        remote(v_ref.at[0, pl.ds(2 * other, 2)], vbuf.at[c], ssem.at[2], rsem.at[2], p, sib),
        remote(flag_out, flag.at[c], ssem.at[3], rsem.at[3], p, sib),
    ]
    for copy in swap:
        copy.start()
    tail_copy = remote(tail_out, tail.at[c], ssem.at[5], rsem.at[5], p, sib)
    tail_copy.start()


    for dy, dx in reversed(HOPS):
        base = lax.rem(y + dy, 4) * 8 + lax.rem(x + dx, 4) * 2
        for core in range(2):
            if (dy, dx) != (0, 0):
                remote(
                    qsend.at[pl.ds(2 * core, 2)], qbuf.at[s], ssem.at[0], qrsem.at[y], p, base + core
                ).start()
    remote(qsend.at[pl.ds(2 * other, 2)], qbuf.at[s], ssem.at[0], qrsem.at[y], p, sib).start()
    pltpu.make_async_copy(qsend.at[pl.ds(2 * c, 2)], qbuf.at[s], qrsem.at[y]).start()
    for n in (1, 2, 3):
        swap[n - 1].wait_recv()
    for j in range(2):
        vt[j, other] = jnp.transpose(vbuf[other, j])
    tail_copy.wait_recv()

    def partial(kk, j):
        chunk = lax.rem(y + kk, 4)
        rows = qbuf[pl.ds(8 * chunk, 8), j].reshape(128, 128)
        tops, sums, outs = [], [], []
        for core in range(2):
            scores = dot(kbuf[core, j], rows, NT) * SCALE
            for slot in range(2):
                block = scores[128 * slot : 128 * slot + 128]
                block_max = jnp.max(block, axis=0, keepdims=True)
                e = jnp.exp(block - block_max)
                sums.append(jnp.sum(e, axis=0, keepdims=True))
                outs.append(dot(vt[j, core, :, 128 * slot : 128 * slot + 128], e.astype(bf16)))
                if slot == 1:
                    live = flag[core, j : j + 1, :] > 1.5
                    block_max = jnp.where(live, block_max, NEGATIVE)
                tops.append(block_max)
        if kk == 0:
            for core in range(2):
                mine = lax.div(lane, 16) == 2 * x + core
                tops.append(jnp.where(mine, tail[core, j, 128:129], NEGATIVE))
                sums.append(tail[core, j, 129:130])
                outs.append(tail[core, j, :128])
        top = functools.reduce(jnp.maximum, tops).astype(bf16).astype(f32)
        total, summed = 0.0, 0.0
        for m, t, o in zip(tops, sums, outs):
            factor = jnp.exp(m - top)
            total = total + factor * t
            summed = summed + factor * o
        high = total.astype(bf16).astype(f32)
        stats = jnp.where(row16 == 0, top, jnp.where(row16 == 1, high, total - high))
        stats = stats.astype(bf16)
        summed = summed.astype(bf16)
        for half in range(2):
            part[kk, j, half, :64] = summed[64 * half : 64 * half + 64]
            part[kk, j, half, 64:] = stats

    for kk in (0, 1, 3, 2):
        chunk = lax.rem(y + kk, 4)
        wait_bytes(qbuf.at[pl.ds(8 * chunk, 8)], qrsem.at[chunk])
        for j in range(2):
            partial(kk, j)
        for j in range(2):
            for half in range(2):
                send_or_keep(
                    part.at[kk, j, half], rbuf.at[chip], 6, (2 * c + j) * 8 + chunk * 2 + half
                )

    pl.semaphore_wait(known.at[0], 2)
    spread(1, 4)

    wait_bytes(rbuf, rsem.at[6])
    for dx in (2, 1, 3):
        remote(
            w_ref, wbuf.at[c, :, x], ssem.at[4], rsem.at[4], p, y * 8 + lax.rem(x + dx, 4) * 2 + c
        ).start()
    pltpu.make_async_copy(w_ref, wbuf.at[c, :, x], rsem.at[4]).start()

    tops = [rbuf[k, 64:80].astype(f32) for k in range(16)]
    top = functools.reduce(jnp.maximum, [t[0:1] for t in tops])
    total, summed = 0.0, 0.0
    for k in range(16):
        factor = jnp.exp(tops[k][0:1] - top)
        total = total + factor * (tops[k][1:2] + tops[k][2:3])
        summed = summed + factor * rbuf[k, :64].astype(f32)
    head_out = (summed / total).astype(bf16)
    blank = jnp.zeros_like(head_out)
    stacked = jnp.concatenate(
        [jnp.concatenate([head_out, blank], axis=1), jnp.concatenate([blank, head_out], axis=1)],
        axis=0,
    )
    a, b = iota((64, 256), 0), iota((64, 256), 1)
    place = 2 * lax.div(a, 16) + lax.div(b, 128)
    wanted = lax.rem(a, 16) * 8 + 2 * lax.rem(place, 4) + lax.div(place, 4)
    pick = jnp.where(lax.rem(b, 128) == wanted, 1.0, 0.0).astype(bf16)
    laid = dot(pick, stacked, NT).astype(bf16)
    for g in range(4):
        laid_ref[:, 128 * g : 128 * g + 128] = laid[16 * g : 16 * g + 16]

    pl.semaphore_wait(known.at[1], 2)
    parity = lax.rem(p, 2)
    own_slot = zbuf.at[lax.div(p, 2)]
    for o in DIRECT:
        remote(
            laid_ref, own_slot.at[c], zssem.at[0], zrsem.at[lax.div(p, 2)], zoff(o), s - c + parity
        ).start()

    @pl.when(c == parity)
    def _():
        pltpu.make_async_copy(laid_ref, own_slot.at[c], zrsem.at[lax.div(p, 2)]).start()

    @pl.when(c != parity)
    def _():
        remote(laid_ref, own_slot.at[c], zssem.at[1], zrsem.at[lax.div(p, 2)], p, sib).start()

    def zwait(q):
        wait_bytes(zbuf.at[lax.div(q, 2)], zrsem.at[lax.div(q, 2)])

    def relay(source, onward):
        for sign in (1, -1):
            q = zoff(-sign * source)
            zwait(q)
            slot = lax.div(q, 2)
            for o in onward:
                remote(
                    zbuf.at[slot], zbuf.at[slot], zssem.at[2], zrsem.at[slot], zoff(sign * o), s
                ).start()

    odd = lax.rem(p + c, 2)

    @pl.when(odd == 1)
    def _():
        relay(5, (2, 1, -1))

    @pl.when(odd == 0)
    def _():
        relay(2, (1,))

    wait_bytes(wbuf.at[c], rsem.at[4])
    remote(wbuf.at[c], wbuf.at[c], ssem.at[7], rsem.at[8], p, sib).start()

    wait_bytes(wbuf.at[other], rsem.at[8])
    mine = lax.rem(x, 2) * 4 + y
    near = (5 * odd + 2 * (1 - odd), -5 * odd - 2 * (1 - odd), odd, 8 - 9 * odd)
    far = (3 * odd + 4 * (1 - odd), -3 * odd - 4 * (1 - odd), 7 * odd + 6 * (1 - odd), -7 * odd - 6 * (1 - odd))
    for n, group in enumerate((near, far)):
        planes = [zoff(o) for o in group]
        for q in planes[2:] if n == 0 else planes:
            zwait(q)
        terms = 0.0
        for half in range(2):
            rows = jnp.concatenate([zbuf[lax.div(q, 2), half] for q in planes], axis=0)
            for core in range(2):
                terms = terms + dot(
                    rows[:, 256 * core : 256 * core + 256], wbuf[core, half].reshape(256, 512)
                )
        psend[4 * n : 4 * n + 4] = terms.astype(bf16).reshape(4, 16, 512)
        for k, q in enumerate(planes):
            send_or_keep(psend.at[4 * n + k], obuf.at[mine], 9, 2 * q + lax.div(x, 2))
    wait_bytes(obuf, rsem.at[9])
    wait_bytes(qbuf.at[pl.ds(0, 31)], ssem.at[0])
    for copy in swap:
        copy.wait_send()
    tail_copy.wait_send()
    wait_bytes(wbuf.at[0, :, pl.ds(0, 3)], ssem.at[4])
    wait_bytes(rbuf.at[pl.ds(0, 15)], ssem.at[6])

    @pl.when(lax.div(y, 2) != c)
    def _():
        wait_bytes(rbuf.at[15], ssem.at[6])

    wait_bytes(wbuf.at[0], ssem.at[7])
    wait_bytes(zbuf.at[pl.ds(0, len(DIRECT)), 0], zssem.at[0])

    @pl.when(c != parity)
    def _():
        wait_bytes(laid_ref, zssem.at[1])

    wait_bytes(zbuf.at[pl.ds(0, 2)], zssem.at[2])

    @pl.when(odd == 1)
    def _():
        wait_bytes(zbuf.at[pl.ds(0, 4)], zssem.at[2])

    wait_bytes(obuf.at[pl.ds(0, 7)], ssem.at[9])

    @pl.when(x != 3 * c)
    def _():
        wait_bytes(obuf.at[7], ssem.at[9])


def on_device(*args):
    args = list(args)
    args[3] = jnp.transpose(args[3], (0, 2, 1))
    args[9] = args[9].reshape(2, 64, 512)
    terms = pl.pallas_call(
        kernel,
        out_shape=jax.ShapeDtypeStruct((8, 16, 512), bf16),
        in_specs=[pl.BlockSpec(memory_space=pltpu.HBM)] * 10,
        out_specs=pl.BlockSpec(memory_space=pltpu.HBM),
        scratch_shapes=[
            pltpu.VMEM((2, 32, 128), bf16),
            pltpu.VMEM((4, 16, 128), bf16),
            pltpu.VMEM((32, 2, 16, 128), bf16),
            pltpu.VMEM((2, 2, 256, 128), bf16),
            pltpu.VMEM((2, 2, 256, 128), bf16),
            pltpu.VMEM((2, 2, 128, 256), bf16),
            pltpu.VMEM((4, 256, 128), bf16),
            pltpu.VMEM((4, 256, 128), bf16),
            pltpu.VMEM((2, 4, 128), bf16),
            pltpu.VMEM((2, 4, 128), bf16),
            pltpu.VMEM((8, 128), f32),
            pltpu.VMEM((2, 8, 128), f32),
            pltpu.VMEM((4, 128, 128), bf16),
            pltpu.VMEM((2, 136, 128), f32),
            pltpu.VMEM((2, 2, 136, 128), f32),
            pltpu.VMEM((4, 2, 2, 80, 128), bf16),
            pltpu.VMEM((16, 80, 128), bf16),
            pltpu.VMEM((16, 512), bf16),
            pltpu.VMEM((8, 2, 16, 512), bf16),
            pltpu.VMEM((2, 2, 4, 64, 512), bf16),
            pltpu.VMEM((8, 16, 512), bf16),
            pltpu.SMEM((1, 1, 4), jnp.int32),
            pltpu.SMEM((1, 1), jnp.int32),
            pltpu.SemaphoreType.DMA((9,)),
            pltpu.SemaphoreType.DMA((10,)),
            pltpu.SemaphoreType.DMA((10,)),
            pltpu.SemaphoreType.DMA((3,)),
            pltpu.SemaphoreType.DMA((8,)),
            pltpu.SemaphoreType.DMA((4,)),
            pltpu.SemaphoreType.REGULAR((2,)),
        ],
        compiler_params=pltpu.CompilerParams(
            collective_id=0, has_side_effects=True, vmem_limit_bytes=56 * 1024 * 1024
        ),
        name="attend",
    )(*args)
    terms = terms.reshape(2, 4, 16, 512).astype(f32)
    return jnp.sum(terms, axis=1).reshape(32, 512).astype(bf16)


def solution(mesh):
    placed = (
        P("prompt", "seq", None, None, None),
        P("prompt", None, "seq", None),
        P("prompt", None, "seq", None),
        P("prompt", None, "seq"),
        P("prompt", "seq", None, None, None),
        P("prompt", "seq", None, None, None),
        P("prompt", "seq"),
        P("prompt", "seq", None, None, None),
        P("prompt", "seq", None, None, None),
        P("seq", "prompt"),
    )
    return jax.shard_map(
        on_device, mesh=mesh, in_specs=placed, out_specs=P("seq", "prompt"), check_vma=False
    )
```

```python
import functools
import math

import jax
import jax.numpy as jnp
from jax import lax
from jax.experimental import pallas as pl
from jax.experimental.pallas import tpu as pltpu
from jax.sharding import PartitionSpec as P

MESH = pl.DeviceIdType.MESH
bf16 = jnp.bfloat16
f32 = jnp.float32
NEGATIVE = -1e30

NP = 16
NS = 32
SCALE = 1.0 / math.sqrt(128)
DIRECT = (5, -5, 8, 2, -2, 1, -1)
HOPS = sorted(
    ((dy, dx) for dy in range(4) for dx in range(4)),
    key=lambda t: -(min(t[0], 4 - t[0]) + min(t[1], 4 - t[1])),
)
NT = (((1,), (1,)), ((), ()))
TN = (((0,), (0,)), ((), ()))


def dot(a, b, dims=(((1,), (0,)), ((), ()))):
    return lax.dot_general(a, b, dims, preferred_element_type=f32)


def iota(shape, axis):
    return lax.broadcasted_iota(jnp.int32, shape, axis)


def kernel(
    q_ref, k_ref, v_ref, kept_hbm, sk_ref, sv_ref, len_hbm, dk_ref, dv_ref, w_ref,
    obuf,
    qv, qsend, qbuf, kbuf, vbuf, vt, skv, svv, dkv, dvv, flag_out, flag, qpl,
    tail_out, tail, part, rbuf, laid_ref, zbuf, wbuf, psend,
    kept_ref, len_ref, lsem, ssem, rsem, zssem, zrsem, qrsem, known,
):
    p, s = lax.axis_index("prompt"), lax.axis_index("seq")
    y, i = lax.div(s, 8), lax.rem(s, 8)
    x, c = lax.div(i, 2), lax.rem(s, 2)
    chip, other = lax.div(s, 2), 1 - c
    sib = s + 1 - 2 * c

    def at(plane, seq):
        return {"prompt": plane, "seq": seq}

    def zoff(o):
        return lax.rem(p + o + NP, NP)

    def remote(src, dst, send, recv, plane, seq):
        return pltpu.make_async_remote_copy(
            src, dst, send, recv, device_id=at(plane, seq), device_id_type=MESH
        )

    def wait_bytes(ref, sem):
        pltpu.make_async_copy(ref, ref, sem).wait()

    def send_or_keep(src, dst, n, seq):
        own = seq == s

        @pl.when(own)
        def _():
            pltpu.make_async_copy(src, dst, rsem.at[n]).start()

        @pl.when(jnp.logical_not(own))
        def _():
            remote(src, dst, ssem.at[n], rsem.at[n], p, seq).start()

    local = [
        pltpu.make_async_copy(q_ref.at[0, 0], qv, lsem.at[0]),
        pltpu.make_async_copy(sk_ref.at[0, 0], skv, lsem.at[1]),
        pltpu.make_async_copy(dk_ref.at[0, 0], dkv, lsem.at[2]),
        pltpu.make_async_copy(sv_ref.at[0, 0], svv, lsem.at[3]),
        pltpu.make_async_copy(dv_ref.at[0, 0], dvv, lsem.at[4]),
        pltpu.make_async_copy(k_ref.at[0, pl.ds(2 * c, 2)], kbuf.at[c], lsem.at[5]),
        pltpu.make_async_copy(v_ref.at[0, pl.ds(2 * c, 2)], vbuf.at[c], lsem.at[6]),
        pltpu.make_async_copy(kept_hbm, kept_ref, lsem.at[7]),
        pltpu.make_async_copy(len_hbm, len_ref, lsem.at[8]),
    ]
    for copy in local:
        copy.start()

    barrier = pltpu.get_barrier_semaphore()

    def greet(k, carry):
        pl.semaphore_signal(
            barrier, inc=1, device_id=at(p, lax.rem(s + k, NS)), device_id_type=MESH
        )
        return carry

    lax.fori_loop(1, NS, greet, 0)
    for o in (2, -2, 1, -1):
        for seq in (s, sib):
            pl.semaphore_signal(barrier, inc=1, device_id=at(zoff(o), seq), device_id_type=MESH)

    local[0].wait()
    heads = qv[...].astype(f32).reshape(2, 4, 8, 128)
    for h in range(4):
        rows = heads[:, h].reshape(16, 128).astype(bf16)
        qsend[h] = rows
    row8 = iota((8, 128), 0)

    def flags(core):
        first = kept_ref[0, 0, 2 * core].astype(f32)
        second = kept_ref[0, 0, 2 * core + 1].astype(f32)
        return jnp.where(row8 == 0, first, second)

    local[7].wait()
    flag[c] = flags(c)
    flag_out[...] = flags(other)

    lane = iota((1, 128), 1)
    qpl[...] = jnp.zeros((4, 128, 128), bf16)
    for h in range(4):
        qpl[h, pl.ds(pl.multiple_of(16 * i, 16), 16), :] = qsend[h]
    for copy in local[1:5] + local[8:]:
        copy.wait()
    placed = qpl[...].reshape(512, 128)
    fresh = [dot(dkv[u], placed, NT) * SCALE for u in range(2)]
    later_step = lax.rem(lax.div(lane, 8), 2) == 1
    key_mask = iota((256, 128), 0) < len_ref[0, 0]
    row16 = iota((16, 128), 0)
    for h in range(4):
        scores = dot(skv[h], qpl[h], NT) * SCALE
        scores = jnp.where(key_mask, scores, NEGATIVE)
        f0 = fresh[0][h : h + 1, 128 * h : 128 * h + 128]
        f1 = jnp.where(later_step, fresh[1][h : h + 1, 128 * h : 128 * h + 128], NEGATIVE)
        top = jnp.maximum(jnp.max(scores, axis=0, keepdims=True), jnp.maximum(f0, f1))
        e = jnp.where(key_mask, jnp.exp(scores - top), 0.0)
        e0, e1 = jnp.exp(f0 - top), jnp.where(later_step, jnp.exp(f1 - top), 0.0)
        total = jnp.sum(e, axis=0, keepdims=True) + e0 + e1
        value0 = dvv[0].astype(f32)[h : h + 1]
        value1 = dvv[1].astype(f32)[h : h + 1]
        values = jnp.where(row16 == 0, value0, jnp.where(row16 == 1, value1, 0.0)).astype(bf16)
        weights = jnp.where(row16 == 0, e0, jnp.where(row16 == 1, e1, 0.0)).astype(bf16)
        o = dot(svv[h], e.astype(bf16), TN) + dot(values, weights, TN)
        stats = jnp.where(row8 == 0, top, total)
        core, j = h // 2, h % 2

        @pl.when(c == core)
        def _():
            tail[c, j, :128] = o
            tail[c, j, 128:] = stats

        @pl.when(c != core)
        def _():
            tail_out[j, :128] = o
            tail_out[j, 128:] = stats

    local[5].wait()
    local[6].wait()
    for j in range(2):
        vt[j, c] = jnp.transpose(vbuf[c, j])

    pl.semaphore_wait(barrier, NS - 1 + 8)

    def spread(n, o):
        for sign in (1, -1):
            pl.semaphore_signal(
                known.at[n], inc=1, device_id=at(zoff(sign * o), s), device_id_type=MESH
            )

    spread(0, 2)

    swap = [
        remote(k_ref.at[0, pl.ds(2 * other, 2)], kbuf.at[c], ssem.at[1], rsem.at[1], p, sib),
        remote(v_ref.at[0, pl.ds(2 * other, 2)], vbuf.at[c], ssem.at[2], rsem.at[2], p, sib),
        remote(flag_out, flag.at[c], ssem.at[3], rsem.at[3], p, sib),
    ]
    for copy in swap:
        copy.start()
    tail_copy = remote(tail_out, tail.at[c], ssem.at[5], rsem.at[5], p, sib)
    tail_copy.start()


    for dy, dx in reversed(HOPS):
        base = lax.rem(y + dy, 4) * 8 + lax.rem(x + dx, 4) * 2
        for core in range(2):
            if (dy, dx) != (0, 0):
                remote(
                    qsend.at[pl.ds(2 * core, 2)], qbuf.at[s], ssem.at[0], qrsem.at[y], p, base + core
                ).start()
    remote(qsend.at[pl.ds(2 * other, 2)], qbuf.at[s], ssem.at[0], qrsem.at[y], p, sib).start()
    pltpu.make_async_copy(qsend.at[pl.ds(2 * c, 2)], qbuf.at[s], qrsem.at[y]).start()
    for n in (1, 2, 3):
        swap[n - 1].wait_recv()
    for j in range(2):
        vt[j, other] = jnp.transpose(vbuf[other, j])
    tail_copy.wait_recv()

    def partial(kk, j):
        chunk = lax.rem(y + kk, 4)
        rows = qbuf[pl.ds(8 * chunk, 8), j].reshape(128, 128)
        tops, sums, outs = [], [], []
        for core in range(2):
            scores = dot(kbuf[core, j], rows, NT) * SCALE
            for slot in range(2):
                block = scores[128 * slot : 128 * slot + 128]
                block_max = jnp.max(block, axis=0, keepdims=True)
                e = jnp.exp(block - block_max)
                sums.append(jnp.sum(e, axis=0, keepdims=True))
                outs.append(dot(vt[j, core, :, 128 * slot : 128 * slot + 128], e.astype(bf16)))
                if slot == 1:
                    live = flag[core, j : j + 1, :] > 1.5
                    block_max = jnp.where(live, block_max, NEGATIVE)
                tops.append(block_max)
        if kk == 0:
            for core in range(2):
                mine = lax.div(lane, 16) == 2 * x + core
                tops.append(jnp.where(mine, tail[core, j, 128:129], NEGATIVE))
                sums.append(tail[core, j, 129:130])
                outs.append(tail[core, j, :128])
        top = functools.reduce(jnp.maximum, tops).astype(bf16).astype(f32)
        total, summed = 0.0, 0.0
        for m, t, o in zip(tops, sums, outs):
            factor = jnp.exp(m - top)
            total = total + factor * t
            summed = summed + factor * o
        high = total.astype(bf16).astype(f32)
        stats = jnp.where(row16 == 0, top, jnp.where(row16 == 1, high, total - high))
        stats = stats.astype(bf16)
        summed = summed.astype(bf16)
        for half in range(2):
            part[kk, j, half, :64] = summed[64 * half : 64 * half + 64]
            part[kk, j, half, 64:] = stats

    for kk in (0, 1, 3, 2):
        chunk = lax.rem(y + kk, 4)
        wait_bytes(qbuf.at[pl.ds(8 * chunk, 8)], qrsem.at[chunk])
        for j in range(2):
            partial(kk, j)
        for j in range(2):
            for half in range(2):
                send_or_keep(
                    part.at[kk, j, half], rbuf.at[chip], 6, (2 * c + j) * 8 + chunk * 2 + half
                )

    pl.semaphore_wait(known.at[0], 2)
    spread(1, 4)

    wait_bytes(rbuf, rsem.at[6])
    for dx in (2, 1, 3):
        remote(
            w_ref, wbuf.at[c, :, x], ssem.at[4], rsem.at[8 if dx == 2 else 4], p,
            y * 8 + lax.rem(x + dx, 4) * 2 + c,
        ).start()
    pltpu.make_async_copy(w_ref, wbuf.at[c, :, x], lsem.at[9]).start()
    remote(w_ref, wbuf.at[c, :, x], ssem.at[7], rsem.at[7], p, sib).start()

    tops = [rbuf[k, 64:80].astype(f32) for k in range(16)]
    top = functools.reduce(jnp.maximum, [t[0:1] for t in tops])
    total, summed = 0.0, 0.0
    for k in range(16):
        factor = jnp.exp(tops[k][0:1] - top)
        total = total + factor * (tops[k][1:2] + tops[k][2:3])
        summed = summed + factor * rbuf[k, :64].astype(f32)
    head_out = (summed / total).astype(bf16)
    blank = jnp.zeros_like(head_out)
    stacked = jnp.concatenate(
        [jnp.concatenate([head_out, blank], axis=1), jnp.concatenate([blank, head_out], axis=1)],
        axis=0,
    )
    a, b = iota((64, 256), 0), iota((64, 256), 1)
    place = 2 * lax.div(a, 16) + lax.div(b, 128)
    wanted = lax.rem(a, 16) * 8 + 2 * lax.rem(place, 4) + lax.div(place, 4)
    pick = jnp.where(lax.rem(b, 128) == wanted, 1.0, 0.0).astype(bf16)
    laid = dot(pick, stacked, NT).astype(bf16)
    for g in range(4):
        laid_ref[:, 128 * g : 128 * g + 128] = laid[16 * g : 16 * g + 16]

    pl.semaphore_wait(known.at[1], 2)
    parity = lax.rem(p, 2)
    own_slot = zbuf.at[lax.div(p, 2)]
    for o in DIRECT:
        remote(
            laid_ref, own_slot.at[c], zssem.at[0], zrsem.at[lax.div(p, 2)], zoff(o), s - c + parity
        ).start()

    @pl.when(c == parity)
    def _():
        pltpu.make_async_copy(laid_ref, own_slot.at[c], zrsem.at[lax.div(p, 2)]).start()

    @pl.when(c != parity)
    def _():
        remote(laid_ref, own_slot.at[c], zssem.at[1], zrsem.at[lax.div(p, 2)], p, sib).start()

    def zwait(q):
        wait_bytes(zbuf.at[lax.div(q, 2)], zrsem.at[lax.div(q, 2)])

    def relay(source, onward):
        for sign in (1, -1):
            q = zoff(-sign * source)
            zwait(q)
            slot = lax.div(q, 2)
            for o in onward:
                remote(
                    zbuf.at[slot], zbuf.at[slot], zssem.at[2], zrsem.at[slot], zoff(sign * o), s
                ).start()

    odd = lax.rem(p + c, 2)

    @pl.when(odd == 1)
    def _():
        relay(5, (2, 1, -1))

    @pl.when(odd == 0)
    def _():
        relay(2, (1,))

    def forward(dx):
        block = wbuf.at[c, :, lax.rem(x + dx, 4)]
        remote(block, block, ssem.at[7], rsem.at[7], p, sib).start()

    wait_bytes(wbuf.at[c, :, pl.ds(0, 2)], rsem.at[4])
    forward(1)
    forward(3)
    wait_bytes(wbuf.at[c, :, 0], rsem.at[8])
    forward(2)
    wait_bytes(wbuf.at[c, :, 0], lsem.at[9])

    wait_bytes(wbuf.at[other], rsem.at[7])
    mine = lax.rem(x, 2) * 4 + y
    near = (5 * odd + 2 * (1 - odd), -5 * odd - 2 * (1 - odd), odd, 8 - 9 * odd)
    middle = (3 * odd + 4 * (1 - odd), -3 * odd - 4 * (1 - odd))
    far = (7 * odd + 6 * (1 - odd), -7 * odd - 6 * (1 - odd))
    done = 0
    for n, group in enumerate((near, middle, far)):
        planes = [zoff(o) for o in group]
        for q in planes[2:] if n == 0 else planes:
            zwait(q)
        terms = 0.0
        for half in range(2):
            rows = jnp.concatenate([zbuf[lax.div(q, 2), half] for q in planes], axis=0)
            for core in range(2):
                terms = terms + dot(
                    rows[:, 256 * core : 256 * core + 256], wbuf[core, half].reshape(256, 512)
                )
        psend[done : done + len(group)] = terms.astype(bf16).reshape(len(group), 16, 512)
        for k, q in enumerate(planes):
            send_or_keep(psend.at[done + k], obuf.at[mine], 9, 2 * q + lax.div(x, 2))
        done += len(group)
    wait_bytes(obuf, rsem.at[9])
    wait_bytes(qbuf.at[pl.ds(0, 31)], ssem.at[0])
    for copy in swap:
        copy.wait_send()
    tail_copy.wait_send()
    wait_bytes(wbuf.at[0, :, pl.ds(0, 3)], ssem.at[4])
    wait_bytes(rbuf.at[pl.ds(0, 15)], ssem.at[6])

    @pl.when(lax.div(y, 2) != c)
    def _():
        wait_bytes(rbuf.at[15], ssem.at[6])

    wait_bytes(wbuf.at[0], ssem.at[7])
    wait_bytes(zbuf.at[pl.ds(0, len(DIRECT)), 0], zssem.at[0])

    @pl.when(c != parity)
    def _():
        wait_bytes(laid_ref, zssem.at[1])

    wait_bytes(zbuf.at[pl.ds(0, 2)], zssem.at[2])

    @pl.when(odd == 1)
    def _():
        wait_bytes(zbuf.at[pl.ds(0, 4)], zssem.at[2])

    wait_bytes(obuf.at[pl.ds(0, 7)], ssem.at[9])

    @pl.when(x != 3 * c)
    def _():
        wait_bytes(obuf.at[7], ssem.at[9])


def on_device(*args):
    args = list(args)
    args[3] = jnp.transpose(args[3], (0, 2, 1))
    args[9] = args[9].reshape(2, 64, 512)
    terms = pl.pallas_call(
        kernel,
        out_shape=jax.ShapeDtypeStruct((8, 16, 512), bf16),
        in_specs=[pl.BlockSpec(memory_space=pltpu.HBM)] * 10,
        out_specs=pl.BlockSpec(memory_space=pltpu.HBM),
        scratch_shapes=[
            pltpu.VMEM((2, 32, 128), bf16),
            pltpu.VMEM((4, 16, 128), bf16),
            pltpu.VMEM((32, 2, 16, 128), bf16),
            pltpu.VMEM((2, 2, 256, 128), bf16),
            pltpu.VMEM((2, 2, 256, 128), bf16),
            pltpu.VMEM((2, 2, 128, 256), bf16),
            pltpu.VMEM((4, 256, 128), bf16),
            pltpu.VMEM((4, 256, 128), bf16),
            pltpu.VMEM((2, 4, 128), bf16),
            pltpu.VMEM((2, 4, 128), bf16),
            pltpu.VMEM((8, 128), f32),
            pltpu.VMEM((2, 8, 128), f32),
            pltpu.VMEM((4, 128, 128), bf16),
            pltpu.VMEM((2, 136, 128), f32),
            pltpu.VMEM((2, 2, 136, 128), f32),
            pltpu.VMEM((4, 2, 2, 80, 128), bf16),
            pltpu.VMEM((16, 80, 128), bf16),
            pltpu.VMEM((16, 512), bf16),
            pltpu.VMEM((8, 2, 16, 512), bf16),
            pltpu.VMEM((2, 2, 4, 64, 512), bf16),
            pltpu.VMEM((8, 16, 512), bf16),
            pltpu.SMEM((1, 1, 4), jnp.int32),
            pltpu.SMEM((1, 1), jnp.int32),
            pltpu.SemaphoreType.DMA((10,)),
            pltpu.SemaphoreType.DMA((10,)),
            pltpu.SemaphoreType.DMA((10,)),
            pltpu.SemaphoreType.DMA((3,)),
            pltpu.SemaphoreType.DMA((8,)),
            pltpu.SemaphoreType.DMA((4,)),
            pltpu.SemaphoreType.REGULAR((2,)),
        ],
        compiler_params=pltpu.CompilerParams(
            collective_id=0, has_side_effects=True, vmem_limit_bytes=56 * 1024 * 1024
        ),
        name="attend",
    )(*args)
    terms = terms.reshape(2, 4, 16, 512).astype(f32)
    return jnp.sum(terms, axis=1).reshape(32, 512).astype(bf16)


def solution(mesh):
    placed = (
        P("prompt", "seq", None, None, None),
        P("prompt", None, "seq", None),
        P("prompt", None, "seq", None),
        P("prompt", None, "seq"),
        P("prompt", "seq", None, None, None),
        P("prompt", "seq", None, None, None),
        P("prompt", "seq"),
        P("prompt", "seq", None, None, None),
        P("prompt", "seq", None, None, None),
        P("seq", "prompt"),
    )
    return jax.shard_map(
        on_device, mesh=mesh, in_specs=placed, out_specs=P("seq", "prompt"), check_vma=False
    )
```

```python
import functools
import math

import jax
import jax.numpy as jnp
from jax import lax
from jax.experimental import pallas as pl
from jax.experimental.pallas import tpu as pltpu
from jax.sharding import PartitionSpec as P

MESH = pl.DeviceIdType.MESH
bf16 = jnp.bfloat16
f32 = jnp.float32
NEGATIVE = -1e30

NP = 16
NS = 32
SCALE = 1.0 / math.sqrt(128)
DIRECT = (5, -5, 8, 2, -2, 1, -1)
HOPS = sorted(
    ((dy, dx) for dy in range(4) for dx in range(4)),
    key=lambda t: -(min(t[0], 4 - t[0]) + min(t[1], 4 - t[1])),
)
NT = (((1,), (1,)), ((), ()))
TN = (((0,), (0,)), ((), ()))


def dot(a, b, dims=(((1,), (0,)), ((), ()))):
    return lax.dot_general(a, b, dims, preferred_element_type=f32)


def iota(shape, axis):
    return lax.broadcasted_iota(jnp.int32, shape, axis)


def kernel(
    q_ref, k_ref, v_ref, kept_hbm, sk_ref, sv_ref, len_hbm, dk_ref, dv_ref, w_ref,
    obuf,
    qv, qsend, qbuf, kbuf, vbuf, vt, skv, svv, dkv, dvv, flag_out, flag, qpl,
    tail_out, tail, part, rbuf, laid_ref, zbuf, wbuf, psend,
    kept_ref, len_ref, lsem, ssem, rsem, zssem, zrsem, qrsem, known,
):
    p, s = lax.axis_index("prompt"), lax.axis_index("seq")
    y, i = lax.div(s, 8), lax.rem(s, 8)
    x, c = lax.div(i, 2), lax.rem(s, 2)
    chip, other = lax.div(s, 2), 1 - c
    sib = s + 1 - 2 * c

    def at(plane, seq):
        return {"prompt": plane, "seq": seq}

    def zoff(o):
        return lax.rem(p + o + NP, NP)

    def remote(src, dst, send, recv, plane, seq):
        return pltpu.make_async_remote_copy(
            src, dst, send, recv, device_id=at(plane, seq), device_id_type=MESH
        )

    def wait_bytes(ref, sem):
        pltpu.make_async_copy(ref, ref, sem).wait()

    def send_or_keep(src, dst, n, seq):
        own = seq == s

        @pl.when(own)
        def _():
            pltpu.make_async_copy(src, dst, rsem.at[n]).start()

        @pl.when(jnp.logical_not(own))
        def _():
            remote(src, dst, ssem.at[n], rsem.at[n], p, seq).start()

    local = [
        pltpu.make_async_copy(q_ref.at[0, 0], qv, lsem.at[0]),
        pltpu.make_async_copy(sk_ref.at[0, 0], skv, lsem.at[1]),
        pltpu.make_async_copy(dk_ref.at[0, 0], dkv, lsem.at[2]),
        pltpu.make_async_copy(sv_ref.at[0, 0], svv, lsem.at[3]),
        pltpu.make_async_copy(dv_ref.at[0, 0], dvv, lsem.at[4]),
        pltpu.make_async_copy(k_ref.at[0, pl.ds(2 * c, 2)], kbuf.at[c], lsem.at[5]),
        pltpu.make_async_copy(v_ref.at[0, pl.ds(2 * c, 2)], vbuf.at[c], lsem.at[6]),
        pltpu.make_async_copy(kept_hbm, kept_ref, lsem.at[7]),
        pltpu.make_async_copy(len_hbm, len_ref, lsem.at[8]),
    ]
    for copy in local:
        copy.start()

    barrier = pltpu.get_barrier_semaphore()

    def greet(k, carry):
        pl.semaphore_signal(
            barrier, inc=1, device_id=at(p, lax.rem(s + k, NS)), device_id_type=MESH
        )
        return carry

    lax.fori_loop(1, NS, greet, 0)
    for o in (2, -2, 1, -1):
        for seq in (s, sib):
            pl.semaphore_signal(barrier, inc=1, device_id=at(zoff(o), seq), device_id_type=MESH)

    local[0].wait()
    heads = qv[...].astype(f32).reshape(2, 4, 8, 128)
    for h in range(4):
        rows = heads[:, h].reshape(16, 128).astype(bf16)
        qsend[h] = rows
    row8 = iota((8, 128), 0)

    def flags(core):
        first = kept_ref[0, 0, 2 * core].astype(f32)
        second = kept_ref[0, 0, 2 * core + 1].astype(f32)
        return jnp.where(row8 == 0, first, second)

    local[7].wait()
    flag[c] = flags(c)
    flag_out[...] = flags(other)

    lane = iota((1, 128), 1)
    qpl[...] = jnp.zeros((4, 128, 128), bf16)
    for h in range(4):
        qpl[h, pl.ds(pl.multiple_of(16 * i, 16), 16), :] = qsend[h]
    for copy in local[1:5] + local[8:]:
        copy.wait()
    placed = qpl[...].reshape(512, 128)
    fresh = [dot(dkv[u], placed, NT) * SCALE for u in range(2)]
    later_step = lax.rem(lax.div(lane, 8), 2) == 1
    key_mask = iota((256, 128), 0) < len_ref[0, 0]
    row16 = iota((16, 128), 0)
    for h in range(4):
        scores = dot(skv[h], qpl[h], NT) * SCALE
        scores = jnp.where(key_mask, scores, NEGATIVE)
        f0 = fresh[0][h : h + 1, 128 * h : 128 * h + 128]
        f1 = jnp.where(later_step, fresh[1][h : h + 1, 128 * h : 128 * h + 128], NEGATIVE)
        top = jnp.maximum(jnp.max(scores, axis=0, keepdims=True), jnp.maximum(f0, f1))
        e = jnp.where(key_mask, jnp.exp(scores - top), 0.0)
        e0, e1 = jnp.exp(f0 - top), jnp.where(later_step, jnp.exp(f1 - top), 0.0)
        total = jnp.sum(e, axis=0, keepdims=True) + e0 + e1
        value0 = dvv[0].astype(f32)[h : h + 1]
        value1 = dvv[1].astype(f32)[h : h + 1]
        values = jnp.where(row16 == 0, value0, jnp.where(row16 == 1, value1, 0.0)).astype(bf16)
        weights = jnp.where(row16 == 0, e0, jnp.where(row16 == 1, e1, 0.0)).astype(bf16)
        o = dot(svv[h], e.astype(bf16), TN) + dot(values, weights, TN)
        stats = jnp.where(row8 == 0, top, total)
        core, j = h // 2, h % 2

        @pl.when(c == core)
        def _():
            tail[c, j, :128] = o
            tail[c, j, 128:] = stats

        @pl.when(c != core)
        def _():
            tail_out[j, :128] = o
            tail_out[j, 128:] = stats

    local[5].wait()
    local[6].wait()
    for j in range(2):
        vt[j, c] = jnp.transpose(vbuf[c, j])

    pl.semaphore_wait(barrier, NS - 1 + 8)

    def spread(n, o):
        for sign in (1, -1):
            pl.semaphore_signal(
                known.at[n], inc=1, device_id=at(zoff(sign * o), s), device_id_type=MESH
            )

    spread(0, 2)

    swap = [
        remote(k_ref.at[0, pl.ds(2 * other, 2)], kbuf.at[c], ssem.at[1], rsem.at[1], p, sib),
        remote(v_ref.at[0, pl.ds(2 * other, 2)], vbuf.at[c], ssem.at[2], rsem.at[2], p, sib),
        remote(flag_out, flag.at[c], ssem.at[3], rsem.at[3], p, sib),
    ]
    for copy in swap:
        copy.start()
    tail_copy = remote(tail_out, tail.at[c], ssem.at[5], rsem.at[5], p, sib)
    tail_copy.start()


    for dy, dx in reversed(HOPS):
        base = lax.rem(y + dy, 4) * 8 + lax.rem(x + dx, 4) * 2
        for core in range(2):
            if (dy, dx) != (0, 0):
                remote(
                    qsend.at[pl.ds(2 * core, 2)], qbuf.at[s], ssem.at[0], qrsem.at[y], p, base + core
                ).start()
    remote(qsend.at[pl.ds(2 * other, 2)], qbuf.at[s], ssem.at[0], qrsem.at[y], p, sib).start()
    pltpu.make_async_copy(qsend.at[pl.ds(2 * c, 2)], qbuf.at[s], qrsem.at[y]).start()
    for n in (1, 2, 3):
        swap[n - 1].wait_recv()
    for j in range(2):
        vt[j, other] = jnp.transpose(vbuf[other, j])
    tail_copy.wait_recv()

    def partial(kk, j):
        chunk = lax.rem(y + kk, 4)
        rows = qbuf[pl.ds(8 * chunk, 8), j].reshape(128, 128)
        tops, sums, outs = [], [], []
        for core in range(2):
            scores = dot(kbuf[core, j], rows, NT) * SCALE
            for slot in range(2):
                block = scores[128 * slot : 128 * slot + 128]
                block_max = jnp.max(block, axis=0, keepdims=True)
                e = jnp.exp(block - block_max)
                sums.append(jnp.sum(e, axis=0, keepdims=True))
                outs.append(dot(vt[j, core, :, 128 * slot : 128 * slot + 128], e.astype(bf16)))
                if slot == 1:
                    live = flag[core, j : j + 1, :] > 1.5
                    block_max = jnp.where(live, block_max, NEGATIVE)
                tops.append(block_max)
        if kk == 0:
            for core in range(2):
                mine = lax.div(lane, 16) == 2 * x + core
                tops.append(jnp.where(mine, tail[core, j, 128:129], NEGATIVE))
                sums.append(tail[core, j, 129:130])
                outs.append(tail[core, j, :128])
        top = functools.reduce(jnp.maximum, tops).astype(bf16).astype(f32)
        total, summed = 0.0, 0.0
        for m, t, o in zip(tops, sums, outs):
            factor = jnp.exp(m - top)
            total = total + factor * t
            summed = summed + factor * o
        high = total.astype(bf16).astype(f32)
        stats = jnp.where(row16 == 0, top, jnp.where(row16 == 1, high, total - high))
        stats = stats.astype(bf16)
        summed = summed.astype(bf16)
        for half in range(2):
            part[kk, j, half, :64] = summed[64 * half : 64 * half + 64]
            part[kk, j, half, 64:] = stats

    for kk in (0, 1, 3, 2):
        chunk = lax.rem(y + kk, 4)
        wait_bytes(qbuf.at[pl.ds(8 * chunk, 8)], qrsem.at[chunk])
        for j in range(2):
            partial(kk, j)
        for j in range(2):
            for half in range(2):
                send_or_keep(
                    part.at[kk, j, half], rbuf.at[chip], 6, (2 * c + j) * 8 + chunk * 2 + half
                )

    pl.semaphore_wait(known.at[0], 2)
    spread(1, 4)

    wait_bytes(rbuf, rsem.at[6])
    for dx in (2, 1, 3):
        remote(
            w_ref, wbuf.at[c, :, x], ssem.at[4], rsem.at[4], p, y * 8 + lax.rem(x + dx, 4) * 2 + c
        ).start()
    pltpu.make_async_copy(w_ref, wbuf.at[c, :, x], rsem.at[4]).start()

    tops = [rbuf[k, 64:80].astype(f32) for k in range(16)]
    top = functools.reduce(jnp.maximum, [t[0:1] for t in tops])
    total, summed = 0.0, 0.0
    for k in range(16):
        factor = jnp.exp(tops[k][0:1] - top)
        total = total + factor * (tops[k][1:2] + tops[k][2:3])
        summed = summed + factor * rbuf[k, :64].astype(f32)
    head_out = (summed / total).astype(bf16)
    blank = jnp.zeros_like(head_out)
    stacked = jnp.concatenate(
        [jnp.concatenate([head_out, blank], axis=1), jnp.concatenate([blank, head_out], axis=1)],
        axis=0,
    )
    a, b = iota((64, 256), 0), iota((64, 256), 1)
    place = 2 * lax.div(a, 16) + lax.div(b, 128)
    wanted = lax.rem(a, 16) * 8 + 2 * lax.rem(place, 4) + lax.div(place, 4)
    pick = jnp.where(lax.rem(b, 128) == wanted, 1.0, 0.0).astype(bf16)
    laid = dot(pick, stacked, NT).astype(bf16)
    for g in range(4):
        laid_ref[:, 128 * g : 128 * g + 128] = laid[16 * g : 16 * g + 16]

    pl.semaphore_wait(known.at[1], 2)
    parity = lax.rem(p, 2)
    own_slot = zbuf.at[lax.div(p, 2)]
    for o in DIRECT:
        remote(
            laid_ref, own_slot.at[c], zssem.at[0], zrsem.at[lax.div(p, 2)], zoff(o), s - c + parity
        ).start()

    @pl.when(c == parity)
    def _():
        pltpu.make_async_copy(laid_ref, own_slot.at[c], zrsem.at[lax.div(p, 2)]).start()

    @pl.when(c != parity)
    def _():
        remote(laid_ref, own_slot.at[c], zssem.at[1], zrsem.at[lax.div(p, 2)], p, sib).start()

    def zwait(q):
        wait_bytes(zbuf.at[lax.div(q, 2)], zrsem.at[lax.div(q, 2)])

    def relay(source, onward):
        slots = []
        for k, o in enumerate(onward):
            for n, sign in enumerate((1, -1)):
                if k == 0:
                    q = zoff(-sign * source)
                    zwait(q)
                    slots.append(lax.div(q, 2))
                slot = slots[n]
                remote(
                    zbuf.at[slot], zbuf.at[slot], zssem.at[2], zrsem.at[slot], zoff(sign * o), s
                ).start()

    odd = lax.rem(p + c, 2)

    @pl.when(odd == 1)
    def _():
        relay(5, (2, 1, -1))

    @pl.when(odd == 0)
    def _():
        relay(2, (1,))

    wait_bytes(wbuf.at[c], rsem.at[4])
    remote(wbuf.at[c], wbuf.at[c], ssem.at[7], rsem.at[8], p, sib).start()

    wait_bytes(wbuf.at[other], rsem.at[8])
    mine = lax.rem(x, 2) * 4 + y
    near = (5 * odd + 2 * (1 - odd), -5 * odd - 2 * (1 - odd), odd, 8 - 9 * odd)
    far = (3 * odd + 4 * (1 - odd), -3 * odd - 4 * (1 - odd), 7 * odd + 6 * (1 - odd), -7 * odd - 6 * (1 - odd))
    for n, group in enumerate((near, far)):
        planes = [zoff(o) for o in group]
        for q in planes[2:] if n == 0 else planes:
            zwait(q)
        terms = 0.0
        for half in range(2):
            rows = jnp.concatenate([zbuf[lax.div(q, 2), half] for q in planes], axis=0)
            for core in range(2):
                terms = terms + dot(
                    rows[:, 256 * core : 256 * core + 256], wbuf[core, half].reshape(256, 512)
                )
        psend[4 * n : 4 * n + 4] = terms.astype(bf16).reshape(4, 16, 512)
        for k, q in enumerate(planes):
            send_or_keep(psend.at[4 * n + k], obuf.at[mine], 9, 2 * q + lax.div(x, 2))
    wait_bytes(obuf, rsem.at[9])
    wait_bytes(qbuf.at[pl.ds(0, 31)], ssem.at[0])
    for copy in swap:
        copy.wait_send()
    tail_copy.wait_send()
    wait_bytes(wbuf.at[0, :, pl.ds(0, 3)], ssem.at[4])
    wait_bytes(rbuf.at[pl.ds(0, 15)], ssem.at[6])

    @pl.when(lax.div(y, 2) != c)
    def _():
        wait_bytes(rbuf.at[15], ssem.at[6])

    wait_bytes(wbuf.at[0], ssem.at[7])
    wait_bytes(zbuf.at[pl.ds(0, len(DIRECT)), 0], zssem.at[0])

    @pl.when(c != parity)
    def _():
        wait_bytes(laid_ref, zssem.at[1])

    wait_bytes(zbuf.at[pl.ds(0, 2)], zssem.at[2])

    @pl.when(odd == 1)
    def _():
        wait_bytes(zbuf.at[pl.ds(0, 4)], zssem.at[2])

    wait_bytes(obuf.at[pl.ds(0, 7)], ssem.at[9])

    @pl.when(x != 3 * c)
    def _():
        wait_bytes(obuf.at[7], ssem.at[9])


def on_device(*args):
    args = list(args)
    args[3] = jnp.transpose(args[3], (0, 2, 1))
    args[9] = args[9].reshape(2, 64, 512)
    terms = pl.pallas_call(
        kernel,
        out_shape=jax.ShapeDtypeStruct((8, 16, 512), bf16),
        in_specs=[pl.BlockSpec(memory_space=pltpu.HBM)] * 10,
        out_specs=pl.BlockSpec(memory_space=pltpu.HBM),
        scratch_shapes=[
            pltpu.VMEM((2, 32, 128), bf16),
            pltpu.VMEM((4, 16, 128), bf16),
            pltpu.VMEM((32, 2, 16, 128), bf16),
            pltpu.VMEM((2, 2, 256, 128), bf16),
            pltpu.VMEM((2, 2, 256, 128), bf16),
            pltpu.VMEM((2, 2, 128, 256), bf16),
            pltpu.VMEM((4, 256, 128), bf16),
            pltpu.VMEM((4, 256, 128), bf16),
            pltpu.VMEM((2, 4, 128), bf16),
            pltpu.VMEM((2, 4, 128), bf16),
            pltpu.VMEM((8, 128), f32),
            pltpu.VMEM((2, 8, 128), f32),
            pltpu.VMEM((4, 128, 128), bf16),
            pltpu.VMEM((2, 136, 128), f32),
            pltpu.VMEM((2, 2, 136, 128), f32),
            pltpu.VMEM((4, 2, 2, 80, 128), bf16),
            pltpu.VMEM((16, 80, 128), bf16),
            pltpu.VMEM((16, 512), bf16),
            pltpu.VMEM((8, 2, 16, 512), bf16),
            pltpu.VMEM((2, 2, 4, 64, 512), bf16),
            pltpu.VMEM((8, 16, 512), bf16),
            pltpu.SMEM((1, 1, 4), jnp.int32),
            pltpu.SMEM((1, 1), jnp.int32),
            pltpu.SemaphoreType.DMA((9,)),
            pltpu.SemaphoreType.DMA((10,)),
            pltpu.SemaphoreType.DMA((10,)),
            pltpu.SemaphoreType.DMA((3,)),
            pltpu.SemaphoreType.DMA((8,)),
            pltpu.SemaphoreType.DMA((4,)),
            pltpu.SemaphoreType.REGULAR((2,)),
        ],
        compiler_params=pltpu.CompilerParams(
            collective_id=0, has_side_effects=True, vmem_limit_bytes=56 * 1024 * 1024
        ),
        name="attend",
    )(*args)
    terms = terms.reshape(2, 4, 16, 512).astype(f32)
    return jnp.sum(terms, axis=1).reshape(32, 512).astype(bf16)


def solution(mesh):
    placed = (
        P("prompt", "seq", None, None, None),
        P("prompt", None, "seq", None),
        P("prompt", None, "seq", None),
        P("prompt", None, "seq"),
        P("prompt", "seq", None, None, None),
        P("prompt", "seq", None, None, None),
        P("prompt", "seq"),
        P("prompt", "seq", None, None, None),
        P("prompt", "seq", None, None, None),
        P("seq", "prompt"),
    )
    return jax.shard_map(
        on_device, mesh=mesh, in_specs=placed, out_specs=P("seq", "prompt"), check_vma=False
    )
```

```python
import functools
import math

import jax
import jax.numpy as jnp
from jax import lax
from jax.experimental import pallas as pl
from jax.experimental.pallas import tpu as pltpu
from jax.sharding import PartitionSpec as P

MESH = pl.DeviceIdType.MESH
bf16 = jnp.bfloat16
f32 = jnp.float32
NEGATIVE = -1e30

NP = 16
NS = 32
SCALE = 1.0 / math.sqrt(128)
DIRECT = (5, -5, 8, 2, -2, 1, -1)
HOPS = sorted(
    ((dy, dx) for dy in range(4) for dx in range(4)),
    key=lambda t: -(min(t[0], 4 - t[0]) + min(t[1], 4 - t[1])),
)
NT = (((1,), (1,)), ((), ()))
TN = (((0,), (0,)), ((), ()))


def dot(a, b, dims=(((1,), (0,)), ((), ()))):
    return lax.dot_general(a, b, dims, preferred_element_type=f32)


def iota(shape, axis):
    return lax.broadcasted_iota(jnp.int32, shape, axis)


def kernel(
    q_ref, k_ref, v_ref, kept_hbm, sk_ref, sv_ref, len_hbm, dk_ref, dv_ref, w_ref,
    obuf,
    qv, qsend, qbuf, kbuf, vbuf, vt, skv, svv, dkv, dvv, flag_out, flag, qpl,
    tail_out, tail, part, rbuf, laid_ref, zbuf, wbuf, psend,
    kept_ref, len_ref, lsem, ssem, rsem, zssem, zrsem, qrsem, prsem, known,
):
    p, s = lax.axis_index("prompt"), lax.axis_index("seq")
    y, i = lax.div(s, 8), lax.rem(s, 8)
    x, c = lax.div(i, 2), lax.rem(s, 2)
    chip, other = lax.div(s, 2), 1 - c
    sib = s + 1 - 2 * c

    def at(plane, seq):
        return {"prompt": plane, "seq": seq}

    def zoff(o):
        return lax.rem(p + o + NP, NP)

    def remote(src, dst, send, recv, plane, seq):
        return pltpu.make_async_remote_copy(
            src, dst, send, recv, device_id=at(plane, seq), device_id_type=MESH
        )

    def wait_bytes(ref, sem):
        pltpu.make_async_copy(ref, ref, sem).wait()

    def send_or_keep(src, dst, n, seq, recv=None):
        recv = rsem.at[n] if recv is None else recv
        own = seq == s

        @pl.when(own)
        def _():
            pltpu.make_async_copy(src, dst, recv).start()

        @pl.when(jnp.logical_not(own))
        def _():
            remote(src, dst, ssem.at[n], recv, p, seq).start()

    local = [
        pltpu.make_async_copy(q_ref.at[0, 0], qv, lsem.at[0]),
        pltpu.make_async_copy(sk_ref.at[0, 0], skv, lsem.at[1]),
        pltpu.make_async_copy(dk_ref.at[0, 0], dkv, lsem.at[2]),
        pltpu.make_async_copy(sv_ref.at[0, 0], svv, lsem.at[3]),
        pltpu.make_async_copy(dv_ref.at[0, 0], dvv, lsem.at[4]),
        pltpu.make_async_copy(k_ref.at[0, pl.ds(2 * c, 2)], kbuf.at[c], lsem.at[5]),
        pltpu.make_async_copy(v_ref.at[0, pl.ds(2 * c, 2)], vbuf.at[c], lsem.at[6]),
        pltpu.make_async_copy(kept_hbm, kept_ref, lsem.at[7]),
        pltpu.make_async_copy(len_hbm, len_ref, lsem.at[8]),
    ]
    for copy in local:
        copy.start()

    barrier = pltpu.get_barrier_semaphore()

    def greet(k, carry):
        pl.semaphore_signal(
            barrier, inc=1, device_id=at(p, lax.rem(s + k, NS)), device_id_type=MESH
        )
        return carry

    lax.fori_loop(1, NS, greet, 0)
    for o in (2, -2, 1, -1):
        for seq in (s, sib):
            pl.semaphore_signal(barrier, inc=1, device_id=at(zoff(o), seq), device_id_type=MESH)

    local[0].wait()
    heads = qv[...].astype(f32).reshape(2, 4, 8, 128)
    for h in range(4):
        rows = heads[:, h].reshape(16, 128).astype(bf16)
        qsend[h] = rows
    row8 = iota((8, 128), 0)

    def flags(core):
        first = kept_ref[0, 0, 2 * core].astype(f32)
        second = kept_ref[0, 0, 2 * core + 1].astype(f32)
        return jnp.where(row8 == 0, first, second)

    local[7].wait()
    flag[c] = flags(c)
    flag_out[...] = flags(other)

    lane = iota((1, 128), 1)
    qpl[...] = jnp.zeros((4, 128, 128), bf16)
    for h in range(4):
        qpl[h, pl.ds(pl.multiple_of(16 * i, 16), 16), :] = qsend[h]
    for copy in local[1:5] + local[8:]:
        copy.wait()
    placed = qpl[...].reshape(512, 128)
    fresh = [dot(dkv[u], placed, NT) * SCALE for u in range(2)]
    later_step = lax.rem(lax.div(lane, 8), 2) == 1
    key_mask = iota((256, 128), 0) < len_ref[0, 0]
    row16 = iota((16, 128), 0)
    for h in range(4):
        scores = dot(skv[h], qpl[h], NT) * SCALE
        scores = jnp.where(key_mask, scores, NEGATIVE)
        f0 = fresh[0][h : h + 1, 128 * h : 128 * h + 128]
        f1 = jnp.where(later_step, fresh[1][h : h + 1, 128 * h : 128 * h + 128], NEGATIVE)
        top = jnp.maximum(jnp.max(scores, axis=0, keepdims=True), jnp.maximum(f0, f1))
        e = jnp.where(key_mask, jnp.exp(scores - top), 0.0)
        e0, e1 = jnp.exp(f0 - top), jnp.where(later_step, jnp.exp(f1 - top), 0.0)
        total = jnp.sum(e, axis=0, keepdims=True) + e0 + e1
        value0 = dvv[0].astype(f32)[h : h + 1]
        value1 = dvv[1].astype(f32)[h : h + 1]
        values = jnp.where(row16 == 0, value0, jnp.where(row16 == 1, value1, 0.0)).astype(bf16)
        weights = jnp.where(row16 == 0, e0, jnp.where(row16 == 1, e1, 0.0)).astype(bf16)
        o = dot(svv[h], e.astype(bf16), TN) + dot(values, weights, TN)
        stats = jnp.where(row8 == 0, top, total)
        core, j = h // 2, h % 2

        @pl.when(c == core)
        def _():
            tail[c, j, :128] = o
            tail[c, j, 128:] = stats

        @pl.when(c != core)
        def _():
            tail_out[j, :128] = o
            tail_out[j, 128:] = stats

    local[5].wait()
    local[6].wait()
    for j in range(2):
        vt[j, c] = jnp.transpose(vbuf[c, j])

    pl.semaphore_wait(barrier, NS - 1 + 8)

    def spread(n, o):
        for sign in (1, -1):
            pl.semaphore_signal(
                known.at[n], inc=1, device_id=at(zoff(sign * o), s), device_id_type=MESH
            )

    spread(0, 2)

    swap = [
        remote(k_ref.at[0, pl.ds(2 * other, 2)], kbuf.at[c], ssem.at[1], rsem.at[1], p, sib),
        remote(v_ref.at[0, pl.ds(2 * other, 2)], vbuf.at[c], ssem.at[2], rsem.at[2], p, sib),
        remote(flag_out, flag.at[c], ssem.at[3], rsem.at[3], p, sib),
    ]
    for copy in swap:
        copy.start()
    tail_copy = remote(tail_out, tail.at[c], ssem.at[5], rsem.at[5], p, sib)
    tail_copy.start()


    for dy, dx in reversed(HOPS):
        base = lax.rem(y + dy, 4) * 8 + lax.rem(x + dx, 4) * 2
        for core in range(2):
            if (dy, dx) != (0, 0):
                remote(
                    qsend.at[pl.ds(2 * core, 2)], qbuf.at[s], ssem.at[0], qrsem.at[y], p, base + core
                ).start()
    remote(qsend.at[pl.ds(2 * other, 2)], qbuf.at[s], ssem.at[0], qrsem.at[y], p, sib).start()
    pltpu.make_async_copy(qsend.at[pl.ds(2 * c, 2)], qbuf.at[s], qrsem.at[y]).start()
    for n in (1, 2, 3):
        swap[n - 1].wait_recv()
    for j in range(2):
        vt[j, other] = jnp.transpose(vbuf[other, j])
    tail_copy.wait_recv()

    def partial(kk, j):
        chunk = lax.rem(y + kk, 4)
        rows = qbuf[pl.ds(8 * chunk, 8), j].reshape(128, 128)
        tops, sums, outs = [], [], []
        for core in range(2):
            scores = dot(kbuf[core, j], rows, NT) * SCALE
            for slot in range(2):
                block = scores[128 * slot : 128 * slot + 128]
                block_max = jnp.max(block, axis=0, keepdims=True)
                e = jnp.exp(block - block_max)
                sums.append(jnp.sum(e, axis=0, keepdims=True))
                outs.append(dot(vt[j, core, :, 128 * slot : 128 * slot + 128], e.astype(bf16)))
                if slot == 1:
                    live = flag[core, j : j + 1, :] > 1.5
                    block_max = jnp.where(live, block_max, NEGATIVE)
                tops.append(block_max)
        if kk == 0:
            for core in range(2):
                mine = lax.div(lane, 16) == 2 * x + core
                tops.append(jnp.where(mine, tail[core, j, 128:129], NEGATIVE))
                sums.append(tail[core, j, 129:130])
                outs.append(tail[core, j, :128])
        top = functools.reduce(jnp.maximum, tops).astype(bf16).astype(f32)
        total, summed = 0.0, 0.0
        for m, t, o in zip(tops, sums, outs):
            factor = jnp.exp(m - top)
            total = total + factor * t
            summed = summed + factor * o
        high = total.astype(bf16).astype(f32)
        stats = jnp.where(row16 == 0, top, jnp.where(row16 == 1, high, total - high))
        stats = stats.astype(bf16)
        summed = summed.astype(bf16)
        for half in range(2):
            part[kk, j, half, :64] = summed[64 * half : 64 * half + 64]
            part[kk, j, half, 64:] = stats

    for kk in (0, 1, 3, 2):
        chunk = lax.rem(y + kk, 4)
        wait_bytes(qbuf.at[pl.ds(8 * chunk, 8)], qrsem.at[chunk])
        for j in range(2):
            partial(kk, j)
        for j in range(2):
            for half in range(2):
                send_or_keep(
                    part.at[kk, j, half], rbuf.at[chip], 6, (2 * c + j) * 8 + chunk * 2 + half,
                    prsem.at[y],
                )

    pl.semaphore_wait(known.at[0], 2)
    spread(1, 4)

    tops, sums, outs = [], [], []
    for dy in (0, 1, 3, 2):
        row = lax.rem(x - dy + 4, 4)
        wait_bytes(rbuf.at[pl.ds(4 * row, 4)], prsem.at[row])
        heads4 = [rbuf[4 * row + k, 64:80].astype(f32) for k in range(4)]
        top = functools.reduce(jnp.maximum, [t[0:1] for t in heads4])
        total, summed = 0.0, 0.0
        for k in range(4):
            factor = jnp.exp(heads4[k][0:1] - top)
            total = total + factor * (heads4[k][1:2] + heads4[k][2:3])
            summed = summed + factor * rbuf[4 * row + k, :64].astype(f32)
        tops.append(top)
        sums.append(total)
        outs.append(summed)
    for dx in (2, 1, 3):
        remote(
            w_ref, wbuf.at[c, :, x], ssem.at[4], rsem.at[4], p, y * 8 + lax.rem(x + dx, 4) * 2 + c
        ).start()
    pltpu.make_async_copy(w_ref, wbuf.at[c, :, x], rsem.at[4]).start()

    top = functools.reduce(jnp.maximum, tops)
    total, summed = 0.0, 0.0
    for m, part_sum, o in zip(tops, sums, outs):
        factor = jnp.exp(m - top)
        total = total + factor * part_sum
        summed = summed + factor * o
    head_out = (summed / total).astype(bf16)
    blank = jnp.zeros_like(head_out)
    stacked = jnp.concatenate(
        [jnp.concatenate([head_out, blank], axis=1), jnp.concatenate([blank, head_out], axis=1)],
        axis=0,
    )
    a, b = iota((64, 256), 0), iota((64, 256), 1)
    place = 2 * lax.div(a, 16) + lax.div(b, 128)
    wanted = lax.rem(a, 16) * 8 + 2 * lax.rem(place, 4) + lax.div(place, 4)
    pick = jnp.where(lax.rem(b, 128) == wanted, 1.0, 0.0).astype(bf16)
    laid = dot(pick, stacked, NT).astype(bf16)
    for g in range(4):
        laid_ref[:, 128 * g : 128 * g + 128] = laid[16 * g : 16 * g + 16]

    pl.semaphore_wait(known.at[1], 2)
    parity = lax.rem(p, 2)
    own_slot = zbuf.at[lax.div(p, 2)]
    for o in DIRECT:
        remote(
            laid_ref, own_slot.at[c], zssem.at[0], zrsem.at[lax.div(p, 2)], zoff(o), s - c + parity
        ).start()

    @pl.when(c == parity)
    def _():
        pltpu.make_async_copy(laid_ref, own_slot.at[c], zrsem.at[lax.div(p, 2)]).start()

    @pl.when(c != parity)
    def _():
        remote(laid_ref, own_slot.at[c], zssem.at[1], zrsem.at[lax.div(p, 2)], p, sib).start()

    def zwait(q):
        wait_bytes(zbuf.at[lax.div(q, 2)], zrsem.at[lax.div(q, 2)])

    def relay(source, onward):
        for sign in (1, -1):
            q = zoff(-sign * source)
            zwait(q)
            slot = lax.div(q, 2)
            for o in onward:
                remote(
                    zbuf.at[slot], zbuf.at[slot], zssem.at[2], zrsem.at[slot], zoff(sign * o), s
                ).start()

    odd = lax.rem(p + c, 2)

    @pl.when(odd == 1)
    def _():
        relay(5, (2, 1, -1))

    @pl.when(odd == 0)
    def _():
        relay(2, (1,))

    wait_bytes(wbuf.at[c], rsem.at[4])
    remote(wbuf.at[c], wbuf.at[c], ssem.at[7], rsem.at[8], p, sib).start()

    wait_bytes(wbuf.at[other], rsem.at[8])
    mine = lax.rem(x, 2) * 4 + y
    near = (5 * odd + 2 * (1 - odd), -5 * odd - 2 * (1 - odd), odd, 8 - 9 * odd)
    far = (3 * odd + 4 * (1 - odd), -3 * odd - 4 * (1 - odd), 7 * odd + 6 * (1 - odd), -7 * odd - 6 * (1 - odd))
    for n, group in enumerate((near, far)):
        planes = [zoff(o) for o in group]
        for q in planes[2:] if n == 0 else planes:
            zwait(q)
        terms = 0.0
        for half in range(2):
            rows = jnp.concatenate([zbuf[lax.div(q, 2), half] for q in planes], axis=0)
            for core in range(2):
                terms = terms + dot(
                    rows[:, 256 * core : 256 * core + 256], wbuf[core, half].reshape(256, 512)
                )
        psend[4 * n : 4 * n + 4] = terms.astype(bf16).reshape(4, 16, 512)
        for k, q in enumerate(planes):
            send_or_keep(psend.at[4 * n + k], obuf.at[mine], 9, 2 * q + lax.div(x, 2))
    wait_bytes(obuf, rsem.at[9])
    wait_bytes(qbuf.at[pl.ds(0, 31)], ssem.at[0])
    for copy in swap:
        copy.wait_send()
    tail_copy.wait_send()
    wait_bytes(wbuf.at[0, :, pl.ds(0, 3)], ssem.at[4])
    wait_bytes(rbuf.at[pl.ds(0, 15)], ssem.at[6])

    @pl.when(lax.div(y, 2) != c)
    def _():
        wait_bytes(rbuf.at[15], ssem.at[6])

    wait_bytes(wbuf.at[0], ssem.at[7])
    wait_bytes(zbuf.at[pl.ds(0, len(DIRECT)), 0], zssem.at[0])

    @pl.when(c != parity)
    def _():
        wait_bytes(laid_ref, zssem.at[1])

    wait_bytes(zbuf.at[pl.ds(0, 2)], zssem.at[2])

    @pl.when(odd == 1)
    def _():
        wait_bytes(zbuf.at[pl.ds(0, 4)], zssem.at[2])

    wait_bytes(obuf.at[pl.ds(0, 7)], ssem.at[9])

    @pl.when(x != 3 * c)
    def _():
        wait_bytes(obuf.at[7], ssem.at[9])


def on_device(*args):
    args = list(args)
    args[3] = jnp.transpose(args[3], (0, 2, 1))
    args[9] = args[9].reshape(2, 64, 512)
    terms = pl.pallas_call(
        kernel,
        out_shape=jax.ShapeDtypeStruct((8, 16, 512), bf16),
        in_specs=[pl.BlockSpec(memory_space=pltpu.HBM)] * 10,
        out_specs=pl.BlockSpec(memory_space=pltpu.HBM),
        scratch_shapes=[
            pltpu.VMEM((2, 32, 128), bf16),
            pltpu.VMEM((4, 16, 128), bf16),
            pltpu.VMEM((32, 2, 16, 128), bf16),
            pltpu.VMEM((2, 2, 256, 128), bf16),
            pltpu.VMEM((2, 2, 256, 128), bf16),
            pltpu.VMEM((2, 2, 128, 256), bf16),
            pltpu.VMEM((4, 256, 128), bf16),
            pltpu.VMEM((4, 256, 128), bf16),
            pltpu.VMEM((2, 4, 128), bf16),
            pltpu.VMEM((2, 4, 128), bf16),
            pltpu.VMEM((8, 128), f32),
            pltpu.VMEM((2, 8, 128), f32),
            pltpu.VMEM((4, 128, 128), bf16),
            pltpu.VMEM((2, 136, 128), f32),
            pltpu.VMEM((2, 2, 136, 128), f32),
            pltpu.VMEM((4, 2, 2, 80, 128), bf16),
            pltpu.VMEM((16, 80, 128), bf16),
            pltpu.VMEM((16, 512), bf16),
            pltpu.VMEM((8, 2, 16, 512), bf16),
            pltpu.VMEM((2, 2, 4, 64, 512), bf16),
            pltpu.VMEM((8, 16, 512), bf16),
            pltpu.SMEM((1, 1, 4), jnp.int32),
            pltpu.SMEM((1, 1), jnp.int32),
            pltpu.SemaphoreType.DMA((9,)),
            pltpu.SemaphoreType.DMA((10,)),
            pltpu.SemaphoreType.DMA((10,)),
            pltpu.SemaphoreType.DMA((3,)),
            pltpu.SemaphoreType.DMA((8,)),
            pltpu.SemaphoreType.DMA((4,)),
            pltpu.SemaphoreType.DMA((4,)),
            pltpu.SemaphoreType.REGULAR((2,)),
        ],
        compiler_params=pltpu.CompilerParams(
            collective_id=0, has_side_effects=True, vmem_limit_bytes=56 * 1024 * 1024
        ),
        name="attend",
    )(*args)
    terms = terms.reshape(2, 4, 16, 512).astype(f32)
    return jnp.sum(terms, axis=1).reshape(32, 512).astype(bf16)


def solution(mesh):
    placed = (
        P("prompt", "seq", None, None, None),
        P("prompt", None, "seq", None),
        P("prompt", None, "seq", None),
        P("prompt", None, "seq"),
        P("prompt", "seq", None, None, None),
        P("prompt", "seq", None, None, None),
        P("prompt", "seq"),
        P("prompt", "seq", None, None, None),
        P("prompt", "seq", None, None, None),
        P("seq", "prompt"),
    )
    return jax.shard_map(
        on_device, mesh=mesh, in_specs=placed, out_specs=P("seq", "prompt"), check_vma=False
    )
```

```python
import functools
import math

import jax
import jax.numpy as jnp
from jax import lax
from jax.experimental import pallas as pl
from jax.experimental.pallas import tpu as pltpu
from jax.sharding import PartitionSpec as P

MESH = pl.DeviceIdType.MESH
bf16 = jnp.bfloat16
f32 = jnp.float32
NEGATIVE = -1e30

NP = 16
NS = 32
SCALE = 1.0 / math.sqrt(128)
DIRECT = (5, -5, 8, 2, -2, 1, -1)
HOPS = sorted(
    ((dy, dx) for dy in range(4) for dx in range(4)),
    key=lambda t: -(min(t[0], 4 - t[0]) + min(t[1], 4 - t[1])),
)
NT = (((1,), (1,)), ((), ()))
TN = (((0,), (0,)), ((), ()))


def dot(a, b, dims=(((1,), (0,)), ((), ()))):
    return lax.dot_general(a, b, dims, preferred_element_type=f32)


def iota(shape, axis):
    return lax.broadcasted_iota(jnp.int32, shape, axis)


def kernel(
    q_ref, k_ref, v_ref, kept_hbm, sk_ref, sv_ref, len_hbm, dk_ref, dv_ref, w_ref,
    obuf,
    qv, qsend, qbuf, kbuf, vbuf, vt, skv, svv, dkv, dvv, flag_out, flag, qpl,
    tail_out, tail, part, rbuf, laid_ref, zbuf, wbuf, psend,
    kept_ref, len_ref, lsem, ssem, rsem, zssem, zrsem, qrsem, prsem, known,
):
    p, s = lax.axis_index("prompt"), lax.axis_index("seq")
    y, i = lax.div(s, 8), lax.rem(s, 8)
    x, c = lax.div(i, 2), lax.rem(s, 2)
    chip, other = lax.div(s, 2), 1 - c
    sib = s + 1 - 2 * c

    def at(plane, seq):
        return {"prompt": plane, "seq": seq}

    def zoff(o):
        return lax.rem(p + o + NP, NP)

    def remote(src, dst, send, recv, plane, seq):
        return pltpu.make_async_remote_copy(
            src, dst, send, recv, device_id=at(plane, seq), device_id_type=MESH
        )

    def wait_bytes(ref, sem):
        pltpu.make_async_copy(ref, ref, sem).wait()

    def send_or_keep(src, dst, n, seq, recv=None):
        recv = rsem.at[n] if recv is None else recv
        own = seq == s

        @pl.when(own)
        def _():
            pltpu.make_async_copy(src, dst, recv).start()

        @pl.when(jnp.logical_not(own))
        def _():
            remote(src, dst, ssem.at[n], recv, p, seq).start()

    local = [
        pltpu.make_async_copy(q_ref.at[0, 0], qv, lsem.at[0]),
        pltpu.make_async_copy(sk_ref.at[0, 0], skv, lsem.at[1]),
        pltpu.make_async_copy(dk_ref.at[0, 0], dkv, lsem.at[2]),
        pltpu.make_async_copy(sv_ref.at[0, 0], svv, lsem.at[3]),
        pltpu.make_async_copy(dv_ref.at[0, 0], dvv, lsem.at[4]),
        pltpu.make_async_copy(k_ref.at[0, pl.ds(2 * c, 2)], kbuf.at[c], lsem.at[5]),
        pltpu.make_async_copy(v_ref.at[0, pl.ds(2 * c, 2)], vbuf.at[c], lsem.at[6]),
        pltpu.make_async_copy(kept_hbm, kept_ref, lsem.at[7]),
        pltpu.make_async_copy(len_hbm, len_ref, lsem.at[8]),
    ]
    for copy in local:
        copy.start()

    barrier = pltpu.get_barrier_semaphore()

    def greet(k, carry):
        pl.semaphore_signal(
            barrier, inc=1, device_id=at(p, lax.rem(s + k, NS)), device_id_type=MESH
        )
        return carry

    lax.fori_loop(1, NS, greet, 0)
    for o in (2, -2, 1, -1):
        for seq in (s, sib):
            pl.semaphore_signal(barrier, inc=1, device_id=at(zoff(o), seq), device_id_type=MESH)

    local[0].wait()
    heads = qv[...].astype(f32).reshape(2, 4, 8, 128)
    for h in range(4):
        rows = heads[:, h].reshape(16, 128).astype(bf16)
        qsend[h] = rows
    row8 = iota((8, 128), 0)

    def flags(core):
        first = kept_ref[0, 0, 2 * core].astype(f32)
        second = kept_ref[0, 0, 2 * core + 1].astype(f32)
        return jnp.where(row8 == 0, first, second)

    local[7].wait()
    flag[c] = flags(c)
    flag_out[...] = flags(other)

    lane = iota((1, 128), 1)
    qpl[...] = jnp.zeros((4, 128, 128), bf16)
    for h in range(4):
        qpl[h, pl.ds(pl.multiple_of(16 * i, 16), 16), :] = qsend[h]
    for copy in local[1:5] + local[8:]:
        copy.wait()
    placed = qpl[...].reshape(512, 128)
    fresh = [dot(dkv[u], placed, NT) * SCALE for u in range(2)]
    later_step = lax.rem(lax.div(lane, 8), 2) == 1
    key_mask = iota((256, 128), 0) < len_ref[0, 0]
    row16 = iota((16, 128), 0)
    for h in range(4):
        scores = dot(skv[h], qpl[h], NT) * SCALE
        scores = jnp.where(key_mask, scores, NEGATIVE)
        f0 = fresh[0][h : h + 1, 128 * h : 128 * h + 128]
        f1 = jnp.where(later_step, fresh[1][h : h + 1, 128 * h : 128 * h + 128], NEGATIVE)
        top = jnp.maximum(jnp.max(scores, axis=0, keepdims=True), jnp.maximum(f0, f1))
        e = jnp.where(key_mask, jnp.exp(scores - top), 0.0)
        e0, e1 = jnp.exp(f0 - top), jnp.where(later_step, jnp.exp(f1 - top), 0.0)
        total = jnp.sum(e, axis=0, keepdims=True) + e0 + e1
        value0 = dvv[0].astype(f32)[h : h + 1]
        value1 = dvv[1].astype(f32)[h : h + 1]
        values = jnp.where(row16 == 0, value0, jnp.where(row16 == 1, value1, 0.0)).astype(bf16)
        weights = jnp.where(row16 == 0, e0, jnp.where(row16 == 1, e1, 0.0)).astype(bf16)
        o = dot(svv[h], e.astype(bf16), TN) + dot(values, weights, TN)
        stats = jnp.where(row8 == 0, top, total)
        core, j = h // 2, h % 2

        @pl.when(c == core)
        def _():
            tail[c, j, :128] = o
            tail[c, j, 128:] = stats

        @pl.when(c != core)
        def _():
            tail_out[j, :128] = o
            tail_out[j, 128:] = stats

    local[5].wait()
    local[6].wait()
    for j in range(2):
        vt[j, c] = jnp.transpose(vbuf[c, j])

    pl.semaphore_wait(barrier, NS - 1 + 8)

    def spread(n, o):
        for sign in (1, -1):
            pl.semaphore_signal(
                known.at[n], inc=1, device_id=at(zoff(sign * o), s), device_id_type=MESH
            )

    spread(0, 2)

    swap = [
        remote(k_ref.at[0, pl.ds(2 * other, 2)], kbuf.at[c], ssem.at[1], rsem.at[1], p, sib),
        remote(v_ref.at[0, pl.ds(2 * other, 2)], vbuf.at[c], ssem.at[2], rsem.at[2], p, sib),
        remote(flag_out, flag.at[c], ssem.at[3], rsem.at[3], p, sib),
    ]
    for copy in swap:
        copy.start()
    tail_copy = remote(tail_out, tail.at[c], ssem.at[5], rsem.at[5], p, sib)
    tail_copy.start()


    for dy, dx in reversed(HOPS):
        base = lax.rem(y + dy, 4) * 8 + lax.rem(x + dx, 4) * 2
        for core in range(2):
            if (dy, dx) != (0, 0):
                remote(
                    qsend.at[pl.ds(2 * core, 2)], qbuf.at[s], ssem.at[0], qrsem.at[y], p, base + core
                ).start()
    remote(qsend.at[pl.ds(2 * other, 2)], qbuf.at[s], ssem.at[0], qrsem.at[y], p, sib).start()
    pltpu.make_async_copy(qsend.at[pl.ds(2 * c, 2)], qbuf.at[s], qrsem.at[y]).start()
    for n in (1, 2, 3):
        swap[n - 1].wait_recv()
    for j in range(2):
        vt[j, other] = jnp.transpose(vbuf[other, j])
    tail_copy.wait_recv()

    def partial(kk, j):
        chunk = lax.rem(y + kk, 4)
        rows = qbuf[pl.ds(8 * chunk, 8), j].reshape(128, 128)
        tops, sums, outs = [], [], []
        for core in range(2):
            scores = dot(kbuf[core, j], rows, NT) * SCALE
            for slot in range(2):
                block = scores[128 * slot : 128 * slot + 128]
                block_max = jnp.max(block, axis=0, keepdims=True)
                e = jnp.exp(block - block_max)
                sums.append(jnp.sum(e, axis=0, keepdims=True))
                outs.append(dot(vt[j, core, :, 128 * slot : 128 * slot + 128], e.astype(bf16)))
                if slot == 1:
                    live = flag[core, j : j + 1, :] > 1.5
                    block_max = jnp.where(live, block_max, NEGATIVE)
                tops.append(block_max)
        if kk == 0:
            for core in range(2):
                mine = lax.div(lane, 16) == 2 * x + core
                tops.append(jnp.where(mine, tail[core, j, 128:129], NEGATIVE))
                sums.append(tail[core, j, 129:130])
                outs.append(tail[core, j, :128])
        top = functools.reduce(jnp.maximum, tops).astype(bf16).astype(f32)
        total, summed = 0.0, 0.0
        for m, t, o in zip(tops, sums, outs):
            factor = jnp.exp(m - top)
            total = total + factor * t
            summed = summed + factor * o
        high = total.astype(bf16).astype(f32)
        stats = jnp.where(row16 == 0, top, jnp.where(row16 == 1, high, total - high))
        stats = stats.astype(bf16)
        summed = summed.astype(bf16)
        for half in range(2):
            part[kk, j, half, :64] = summed[64 * half : 64 * half + 64]
            part[kk, j, half, 64:] = stats

    for kk in (0, 1, 3, 2):
        chunk = lax.rem(y + kk, 4)
        wait_bytes(qbuf.at[pl.ds(8 * chunk, 8)], qrsem.at[chunk])
        for j in range(2):
            partial(kk, j)
        for j in range(2):
            for half in range(2):
                send_or_keep(
                    part.at[kk, j, half], rbuf.at[chip], 6, (2 * c + j) * 8 + chunk * 2 + half,
                    prsem.at[y],
                )

    pl.semaphore_wait(known.at[0], 2)
    spread(1, 4)

    tops, sums, outs = [], [], []
    for dy in (0, 1, 3, 2):
        row = lax.rem(x - dy + 4, 4)
        wait_bytes(rbuf.at[pl.ds(4 * row, 4)], prsem.at[row])
        heads4 = [rbuf[4 * row + k, 64:80].astype(f32) for k in range(4)]
        top = functools.reduce(jnp.maximum, [t[0:1] for t in heads4])
        total, summed = 0.0, 0.0
        for k in range(4):
            factor = jnp.exp(heads4[k][0:1] - top)
            total = total + factor * (heads4[k][1:2] + heads4[k][2:3])
            summed = summed + factor * rbuf[4 * row + k, :64].astype(f32)
        tops.append(top)
        sums.append(total)
        outs.append(summed)
    for dx in (2, 1, 3):
        remote(
            w_ref, wbuf.at[c, :, x], ssem.at[4], rsem.at[8 if dx == 2 else 4], p,
            y * 8 + lax.rem(x + dx, 4) * 2 + c,
        ).start()
    pltpu.make_async_copy(w_ref, wbuf.at[c, :, x], lsem.at[9]).start()
    remote(w_ref, wbuf.at[c, :, x], ssem.at[7], rsem.at[7], p, sib).start()

    top = functools.reduce(jnp.maximum, tops)
    total, summed = 0.0, 0.0
    for m, part_sum, o in zip(tops, sums, outs):
        factor = jnp.exp(m - top)
        total = total + factor * part_sum
        summed = summed + factor * o
    head_out = (summed / total).astype(bf16)
    blank = jnp.zeros_like(head_out)
    stacked = jnp.concatenate(
        [jnp.concatenate([head_out, blank], axis=1), jnp.concatenate([blank, head_out], axis=1)],
        axis=0,
    )
    a, b = iota((64, 256), 0), iota((64, 256), 1)
    place = 2 * lax.div(a, 16) + lax.div(b, 128)
    wanted = lax.rem(a, 16) * 8 + 2 * lax.rem(place, 4) + lax.div(place, 4)
    pick = jnp.where(lax.rem(b, 128) == wanted, 1.0, 0.0).astype(bf16)
    laid = dot(pick, stacked, NT).astype(bf16)
    for g in range(4):
        laid_ref[:, 128 * g : 128 * g + 128] = laid[16 * g : 16 * g + 16]

    pl.semaphore_wait(known.at[1], 2)
    parity = lax.rem(p, 2)
    own_slot = zbuf.at[lax.div(p, 2)]
    for o in DIRECT:
        remote(
            laid_ref, own_slot.at[c], zssem.at[0], zrsem.at[lax.div(p, 2)], zoff(o), s - c + parity
        ).start()

    @pl.when(c == parity)
    def _():
        pltpu.make_async_copy(laid_ref, own_slot.at[c], zrsem.at[lax.div(p, 2)]).start()

    @pl.when(c != parity)
    def _():
        remote(laid_ref, own_slot.at[c], zssem.at[1], zrsem.at[lax.div(p, 2)], p, sib).start()

    def zwait(q):
        wait_bytes(zbuf.at[lax.div(q, 2)], zrsem.at[lax.div(q, 2)])

    def relay(source, onward):
        slots = []
        for k, o in enumerate(onward):
            for n, sign in enumerate((1, -1)):
                if k == 0:
                    q = zoff(-sign * source)
                    zwait(q)
                    slots.append(lax.div(q, 2))
                slot = slots[n]
                remote(
                    zbuf.at[slot], zbuf.at[slot], zssem.at[2], zrsem.at[slot], zoff(sign * o), s
                ).start()

    odd = lax.rem(p + c, 2)

    @pl.when(odd == 1)
    def _():
        relay(5, (2, 1, -1))

    @pl.when(odd == 0)
    def _():
        relay(2, (1,))

    def forward(dx):
        block = wbuf.at[c, :, lax.rem(x + dx, 4)]
        remote(block, block, ssem.at[7], rsem.at[7], p, sib).start()

    wait_bytes(wbuf.at[c, :, pl.ds(0, 2)], rsem.at[4])
    forward(1)
    forward(3)
    wait_bytes(wbuf.at[c, :, 0], rsem.at[8])
    forward(2)
    wait_bytes(wbuf.at[c, :, 0], lsem.at[9])

    wait_bytes(wbuf.at[other], rsem.at[7])
    mine = lax.rem(x, 2) * 4 + y
    near = (5 * odd + 2 * (1 - odd), -5 * odd - 2 * (1 - odd), odd, 8 - 9 * odd)
    far = (3 * odd + 4 * (1 - odd), -3 * odd - 4 * (1 - odd), 7 * odd + 6 * (1 - odd), -7 * odd - 6 * (1 - odd))
    for n, group in enumerate((near, far)):
        planes = [zoff(o) for o in group]
        for q in planes[2:] if n == 0 else planes:
            zwait(q)
        terms = 0.0
        for half in range(2):
            rows = jnp.concatenate([zbuf[lax.div(q, 2), half] for q in planes], axis=0)
            for core in range(2):
                terms = terms + dot(
                    rows[:, 256 * core : 256 * core + 256], wbuf[core, half].reshape(256, 512)
                )
        psend[4 * n : 4 * n + 4] = terms.astype(bf16).reshape(4, 16, 512)
        for k, q in enumerate(planes):
            send_or_keep(psend.at[4 * n + k], obuf.at[mine], 9, 2 * q + lax.div(x, 2))
    wait_bytes(obuf, rsem.at[9])
    wait_bytes(qbuf.at[pl.ds(0, 31)], ssem.at[0])
    for copy in swap:
        copy.wait_send()
    tail_copy.wait_send()
    wait_bytes(wbuf.at[0, :, pl.ds(0, 3)], ssem.at[4])
    wait_bytes(rbuf.at[pl.ds(0, 15)], ssem.at[6])

    @pl.when(lax.div(y, 2) != c)
    def _():
        wait_bytes(rbuf.at[15], ssem.at[6])

    wait_bytes(wbuf.at[0], ssem.at[7])
    wait_bytes(zbuf.at[pl.ds(0, len(DIRECT)), 0], zssem.at[0])

    @pl.when(c != parity)
    def _():
        wait_bytes(laid_ref, zssem.at[1])

    wait_bytes(zbuf.at[pl.ds(0, 2)], zssem.at[2])

    @pl.when(odd == 1)
    def _():
        wait_bytes(zbuf.at[pl.ds(0, 4)], zssem.at[2])

    wait_bytes(obuf.at[pl.ds(0, 7)], ssem.at[9])

    @pl.when(x != 3 * c)
    def _():
        wait_bytes(obuf.at[7], ssem.at[9])


def on_device(*args):
    args = list(args)
    args[3] = jnp.transpose(args[3], (0, 2, 1))
    args[9] = args[9].reshape(2, 64, 512)
    terms = pl.pallas_call(
        kernel,
        out_shape=jax.ShapeDtypeStruct((8, 16, 512), bf16),
        in_specs=[pl.BlockSpec(memory_space=pltpu.HBM)] * 10,
        out_specs=pl.BlockSpec(memory_space=pltpu.HBM),
        scratch_shapes=[
            pltpu.VMEM((2, 32, 128), bf16),
            pltpu.VMEM((4, 16, 128), bf16),
            pltpu.VMEM((32, 2, 16, 128), bf16),
            pltpu.VMEM((2, 2, 256, 128), bf16),
            pltpu.VMEM((2, 2, 256, 128), bf16),
            pltpu.VMEM((2, 2, 128, 256), bf16),
            pltpu.VMEM((4, 256, 128), bf16),
            pltpu.VMEM((4, 256, 128), bf16),
            pltpu.VMEM((2, 4, 128), bf16),
            pltpu.VMEM((2, 4, 128), bf16),
            pltpu.VMEM((8, 128), f32),
            pltpu.VMEM((2, 8, 128), f32),
            pltpu.VMEM((4, 128, 128), bf16),
            pltpu.VMEM((2, 136, 128), f32),
            pltpu.VMEM((2, 2, 136, 128), f32),
            pltpu.VMEM((4, 2, 2, 80, 128), bf16),
            pltpu.VMEM((16, 80, 128), bf16),
            pltpu.VMEM((16, 512), bf16),
            pltpu.VMEM((8, 2, 16, 512), bf16),
            pltpu.VMEM((2, 2, 4, 64, 512), bf16),
            pltpu.VMEM((8, 16, 512), bf16),
            pltpu.SMEM((1, 1, 4), jnp.int32),
            pltpu.SMEM((1, 1), jnp.int32),
            pltpu.SemaphoreType.DMA((10,)),
            pltpu.SemaphoreType.DMA((10,)),
            pltpu.SemaphoreType.DMA((10,)),
            pltpu.SemaphoreType.DMA((3,)),
            pltpu.SemaphoreType.DMA((8,)),
            pltpu.SemaphoreType.DMA((4,)),
            pltpu.SemaphoreType.DMA((4,)),
            pltpu.SemaphoreType.REGULAR((2,)),
        ],
        compiler_params=pltpu.CompilerParams(
            collective_id=0, has_side_effects=True, vmem_limit_bytes=56 * 1024 * 1024
        ),
        name="attend",
    )(*args)
    terms = terms.reshape(2, 4, 16, 512).astype(f32)
    return jnp.sum(terms, axis=1).reshape(32, 512).astype(bf16)


def solution(mesh):
    placed = (
        P("prompt", "seq", None, None, None),
        P("prompt", None, "seq", None),
        P("prompt", None, "seq", None),
        P("prompt", None, "seq"),
        P("prompt", "seq", None, None, None),
        P("prompt", "seq", None, None, None),
        P("prompt", "seq"),
        P("prompt", "seq", None, None, None),
        P("prompt", "seq", None, None, None),
        P("seq", "prompt"),
    )
    return jax.shard_map(
        on_device, mesh=mesh, in_specs=placed, out_specs=P("seq", "prompt"), check_vma=False
    )
```
